256 devices in a mesh: context: 32 (over x_lo, z, core), tensor: 8 (over y, x_hi).
Axes of the slice: x: 4 (x_hi: 2, x_lo: 2; x = x_hi * 2 + x_lo), y: 4, z: 8, core: 2. Of those that a mesh axis runs over, the one named last changes fastest.
Arguments:
- tokens: bfloat16 [40960, 2048], P(('context', 'tensor')), may hold values from -6 to 6
- w_query: bfloat16 [2048, 2048], P(None, 'tensor'), may hold values from -0.125 to 0.125
- w_key: bfloat16 [2048, 2048], P(None, 'tensor'), may hold values from -0.125 to 0.125
- w_value: bfloat16 [2048, 4096], P(None, 'tensor'), may hold values from -0.125 to 0.125
- w_gate_z: bfloat16 [2048, 4096], P(None, 'tensor'), may hold values from -0.125 to 0.125
- w_gates: bfloat16 [2048, 32, 2], P(None, 'tensor'), may hold values from -0.125 to 0.125
- conv_query: bfloat16 [4, 2048], P(None, 'tensor'), may hold values from -3 to 3
- conv_key: bfloat16 [4, 2048], P(None, 'tensor'), may hold values from -3 to 3
- conv_value: bfloat16 [4, 4096], P(None, 'tensor'), may hold values from -3 to 3
- a_log: float32 [32], P('tensor'), may hold values from -11.52 to 0.7
- dt_bias: float32 [32], P('tensor'), may hold values from -4 to -2
- norm_gain: bfloat16 [128], replicated, may hold values from 0.5 to 1.5
- w_out: bfloat16 [4096, 2048], P('tensor'), may hold values from -0.09375 to 0.09375
Outputs:
- mixed: bfloat16 [40960, 2048], P(('context', 'tensor'))
The draws below stay inside these ranges and needn't reach their ends.
All inputs are finite; a program needn't handle non-finite values.
Results may differ from the reference program's by a relative error of at most 0.018.
Values may be sent and summed in bfloat16 or wider, within the bound.
A program may use at most 128 MiB of HBM per device.

```python
import jax
import jax.numpy as jnp
from jax import lax

D = 2048
HK = 16
HV = 32
DK = 128
DV = 128
KW = 4
BLOCK = 64
ROWS_CTX = 1280
TOKENS = 40960
N_CONTEXT = 32
N_TENSOR = 8


def draw_a_log(key, part):
    key = jax.random.fold_in(key, 7)
    pick_key, slow_key, fast_key = jax.random.split(key, 3)
    keep_share = 0.5
    slow_heads = jax.random.uniform(pick_key, (HV,), jnp.float32) < keep_share
    slow_logs = jax.random.uniform(slow_key, (HV,), jnp.float32, -11.51, -7.83)
    fast_logs = jax.random.uniform(fast_key, (HV,), jnp.float32, -1.6, 0.69)
    return jnp.where(slow_heads, slow_logs, fast_logs).astype(jnp.float32)


def block_scale(rng, extent, shards, low, largest):
    factor_of, own = 1.0, jax.random.fold_in(rng, 6)
    for axis_at, blocks in shards:
        steps = jnp.exp(jax.random.uniform(jax.random.fold_in(own, axis_at), (blocks,), jnp.float32, low / len(shards), largest / len(shards)))
        factor_of = factor_of * jnp.repeat(steps, extent[axis_at] // blocks).reshape([-1 if axis == axis_at else 1 for axis in range(len(extent))])
    return factor_of


def bell_draw(key, shape, scale, bound, shards=(), kind=jnp.bfloat16):
    values = scale * jax.random.normal(key, shape, jnp.float32)
    if shards:
        values = values * block_scale(key, shape, shards, -0.22, 0.18)
    return jnp.clip(values, -bound, bound).astype(kind)


def setup_inputs(seed: int = 0) -> dict:
    streams_of = jax.random.split(jax.random.key(seed), 14)
    tokens = bell_draw(streams_of[0], (TOKENS, D), 1.0, 6.0, ((0, 256),))
    w_query = bell_draw(streams_of[1], (D, HK * DK), D ** -0.5, 0.125, ((1, 8),))
    w_key = bell_draw(streams_of[2], (D, HK * DK), D ** -0.5, 0.125, ((1, 8),))
    w_value = bell_draw(streams_of[3], (D, HV * DV), D ** -0.5, 0.125, ((1, 8),))
    w_gate_z = bell_draw(streams_of[4], (D, HV * DV), D ** -0.5, 0.125, ((1, 8),))
    w_gates = bell_draw(streams_of[5], (D, HV, 2), D ** -0.5, 0.125, ((1, 8),))
    conv_query = bell_draw(streams_of[6], (KW, HK * DK), 0.5, 3.0, ((1, 8),))
    conv_key = bell_draw(streams_of[7], (KW, HK * DK), 0.5, 3.0, ((1, 8),))
    conv_value = bell_draw(streams_of[8], (KW, HV * DV), 0.5, 3.0, ((1, 8),))
    a_log = draw_a_log(jax.random.fold_in(streams_of[13], 71), 0)
    dt_bias = jnp.clip(-4.0 + 2.0 * jax.random.uniform(streams_of[10], (HV,), jnp.float32) ** block_scale(streams_of[10], (HV,), ((0, 8),), -0.2, 0.2), -4.0, -2.0)
    norm_gain = jnp.clip(1.0 + 0.1 * jax.random.normal(streams_of[11], (DV,), jnp.float32), 0.5, 1.5).astype(jnp.bfloat16)
    w_out = bell_draw(streams_of[12], (HV * DV, D), (HV * DV) ** -0.5, 0.09375, ((0, 8),))
    return {"tokens": tokens, "w_query": w_query, "w_key": w_key, "w_value": w_value, "w_gate_z": w_gate_z, "w_gates": w_gates, "conv_query": conv_query, "conv_key": conv_key, "conv_value": conv_value, "a_log": a_log, "dt_bias": dt_bias, "norm_gain": norm_gain, "w_out": w_out}


EPSILON = 1e-06
PRECISE = lax.Precision.HIGHEST

def heads_product(left_term, right_term):
    return jnp.einsum('hij,hjk->hik', left_term, right_term, precision=PRECISE)

def block_product(pattern, left_term, right_term):
    return jnp.einsum(pattern, left_term, right_term, precision=PRECISE)

def unit_rows(channels, head_size):
    shaped = channels.reshape(channels.shape[0], -1, head_size)
    return shaped * lax.rsqrt(lax.optimization_barrier(jnp.sum(shaped * shaped, axis=-1, keepdims=True)) + EPSILON)

def causal_conv(earlier, current, kernel):
    extended = jnp.concatenate([earlier, current], axis=0).astype(jnp.float32)
    weights = kernel.astype(jnp.float32)
    count_rows = current.shape[0]
    summed = weights[0] * extended[0:count_rows]
    for offset in range(1, weights.shape[0]):
        summed = summed + weights[offset] * extended[offset:offset + count_rows]
    return jax.nn.silu(summed)

def to_blocks(array, length):
    return array.reshape(array.shape[0] // length, length, array.shape[1], array.shape[2]).transpose(2, 0, 1, 3)

def block_terms(queries, keys, values, decays, strengths, ratio_heads):
    length = keys.shape[2]
    cumulative = jnp.cumsum(decays, axis=-1)
    strict = jnp.tril(jnp.ones((length, length), jnp.float32), -1)
    unit_matrix = jnp.eye(length, dtype=jnp.float32)
    spread = jnp.exp(jnp.minimum(cumulative[..., :, None] - cumulative[..., None, :], 0.0))
    key_key = jnp.repeat(block_product('hbik,hbjk->hbij', keys, keys), ratio_heads, axis=0)
    query_key = jnp.repeat(block_product('hbik,hbjk->hbij', queries, keys), ratio_heads, axis=0)
    keys_wide = jnp.repeat(keys, ratio_heads, axis=0)
    queries_wide = jnp.repeat(queries, ratio_heads, axis=0)
    system = strengths[..., :, None] * spread * strict * key_key + unit_matrix
    growth = jnp.exp(cumulative)
    sources = jnp.concatenate([keys_wide * (strengths * growth)[..., None], values * strengths[..., None]], axis=-1)
    solved = jax.scipy.linalg.solve_triangular(system, sources, lower=True, unit_diagonal=True)
    key_size = keys.shape[-1]
    absorb = solved[..., :key_size]
    written = solved[..., key_size:]
    fading = keys_wide * jnp.exp(cumulative[..., -1:] - cumulative)[..., None]
    key_unit = jnp.eye(key_size, dtype=jnp.float32)
    transfer = growth[..., -1][..., None, None] * key_unit - block_product('hbik,hbil->hbkl', fading, absorb)
    inject = block_product('hbik,hbiv->hbkv', fading, written)
    reach_map = query_key * spread * (strict + unit_matrix)
    scaled_query = queries_wide * growth[..., None]
    return (scaled_query, reach_map, absorb, written, transfer, inject)

def reference(tokens, w_query, w_key, w_value, w_gate_z, w_gates, conv_query, conv_key, conv_value, a_log, dt_bias, norm_gain, w_out):
    margin = KW - 1
    ratio_heads = HV // HK
    group_heads = HV // N_TENSOR
    matrices = (w_query.astype(jnp.float32), w_key.astype(jnp.float32), w_value.astype(jnp.float32), w_gate_z.astype(jnp.float32), w_gates.reshape(D, 2 * HV).astype(jnp.float32))
    out_groups = w_out.astype(jnp.float32).reshape(N_TENSOR, group_heads * DV, D)
    gain = norm_gain.astype(jnp.float32)
    spans = tokens.reshape(N_CONTEXT, ROWS_CTX, D)

    def span_step(carry, block_rows):
        state, tails = carry
        rows_wide = block_rows.astype(jnp.float32)
        projected = tuple((jnp.dot(rows_wide.astype(jnp.float32), matrix.astype(jnp.float32), preferred_element_type=jnp.float32, precision=PRECISE).astype(jnp.bfloat16) for matrix in matrices))
        projected = lax.optimization_barrier(projected)
        pre_query, pre_key, pre_value, gate_z, gate_logits = projected
        conv_q = causal_conv(tails[0], pre_query, conv_query)
        conv_k = causal_conv(tails[1], pre_key, conv_key)
        conv_v = causal_conv(tails[2], pre_value, conv_value)
        new_tails = (pre_query[ROWS_CTX - margin:], pre_key[ROWS_CTX - margin:], pre_value[ROWS_CTX - margin:])
        queries = unit_rows(conv_q, DK) * DK ** (-0.5)
        keys_all = unit_rows(conv_k, DK)
        values_all = conv_v.reshape(ROWS_CTX, HV, DV)
        logits = gate_logits.astype(jnp.float32).reshape(ROWS_CTX, HV, 2)
        decays = -jnp.exp(a_log)[None, :] * jax.nn.softplus(logits[..., 0] + dt_bias[None, :])
        strengths = jax.nn.sigmoid(logits[..., 1])
        count_blocks = ROWS_CTX // BLOCK
        decay_blocks = decays.reshape(count_blocks, BLOCK, HV).transpose(2, 0, 1)
        strength_blocks = strengths.reshape(count_blocks, BLOCK, HV).transpose(2, 0, 1)
        terms = block_terms(to_blocks(queries, BLOCK), to_blocks(keys_all, BLOCK), to_blocks(values_all, BLOCK), decay_blocks, strength_blocks, ratio_heads)
        moved = tuple((jnp.moveaxis(array, 1, 0) for array in terms))

        def advance(current, items):
            query_b, reach_b, absorb_b, written_b, move_b, add_b = items
            fixed = written_b - heads_product(absorb_b, current)
            outputs_b = heads_product(query_b, current) + heads_product(reach_b, fixed)
            return (heads_product(move_b, current) + add_b, outputs_b)
        final_state, core = lax.scan(advance, state, moved)
        core_rows = core.transpose(0, 2, 1, 3).reshape(ROWS_CTX, HV, DV)
        gate_values = gate_z.astype(jnp.float32).reshape(ROWS_CTX, HV, DV)
        mean_square = lax.optimization_barrier(jnp.mean(core_rows * core_rows, axis=-1, keepdims=True))
        normed = (core_rows * lax.rsqrt(mean_square + EPSILON) * gain * jax.nn.silu(gate_values)).reshape(ROWS_CTX, HV * DV).astype(jnp.bfloat16)
        grouped = normed.astype(jnp.float32).reshape(ROWS_CTX, N_TENSOR, group_heads * DV)
        partials = jnp.einsum('rgc,gcd->grd', grouped, out_groups, precision=PRECISE).astype(jnp.bfloat16)
        mixed_rows = lax.optimization_barrier(jnp.sum(partials.astype(jnp.float32), axis=0)).astype(jnp.bfloat16)
        return ((final_state, new_tails), mixed_rows)
    start_state = jnp.zeros((HV, DK, DV), jnp.float32)
    start_tails = (jnp.zeros((margin, HK * DK), jnp.bfloat16), jnp.zeros((margin, HK * DK), jnp.bfloat16), jnp.zeros((margin, HV * DV), jnp.bfloat16))
    unused, outputs = lax.scan(span_step, (start_state, start_tails), spans)
    return outputs.reshape(TOKENS, D)
```

```python
import functools

import jax
import jax.numpy as jnp
from jax import lax
from jax.experimental import pallas as pl
from jax.experimental.pallas import tpu as pltpu
from jax.sharding import PartitionSpec as P

HK = 16
HV = 32
DK = 128
DV = 128
KW = 4
EPSILON = 1e-06
LEN = 128
PER_STEP = 2
HEADS = 4
KEYS = 2
F32 = jnp.float32
B16 = jnp.bfloat16


def mm(a, b):
    return jnp.dot(a, b, preferred_element_type=F32)


def mm_nt(a, b):
    return lax.dot_general(a, b, (((1,), (1,)), ((), ())), preferred_element_type=F32)


def mm_tn(a, b):
    return lax.dot_general(a, b, (((0,), (0,)), ((), ())), preferred_element_type=F32)


def silu(x):
    return x / (1.0 + jnp.exp(-x))


def unit(x):
    return x * lax.rsqrt(jnp.sum(x * x, axis=-1, keepdims=True) + EPSILON)


def chunk_terms(q_all, k_all, v_all, gates, gate_par):
    ii = lax.broadcasted_iota(jnp.int32, (LEN, LEN), 0)
    jj = lax.broadcasted_iota(jnp.int32, (LEN, LEN), 1)
    lower = (ii >= jj).astype(F32)
    strict = (ii > jj).astype(F32)
    differ = ii ^ jj
    levels = [((differ >> s) == 1).astype(B16) for s in range(LEN.bit_length() - 1)]
    eye = (ii == jj).astype(B16)

    logits = gates.astype(F32)
    shifted = logits + gate_par[1:2, :]
    softplus = jnp.maximum(shifted, 0.0) + jnp.log1p(jnp.exp(-jnp.abs(shifted)))
    decays = -jnp.exp(gate_par[0:1, :]) * softplus
    beta = 1.0 / (1.0 + jnp.exp(-logits))
    cum = jnp.dot(lower, decays, preferred_element_type=F32, precision=lax.Precision.HIGHEST)
    cum_t = cum.T
    growth = jnp.exp(cum)
    fade = jnp.exp(cum[LEN - 1 : LEN, :] - cum)

    terms = []
    for g in range(KEYS):
        qf = unit(q_all[:, g * DK : (g + 1) * DK]) * (DK**-0.5)
        kf = unit(k_all[:, g * DK : (g + 1) * DK])
        qb, kb = qf.astype(B16), kf.astype(B16)
        kk = mm_nt(kb, kb) * strict
        qk = mm_nt(qb, kb) * lower
        for h in (2 * g, 2 * g + 1):
            spread = jnp.exp(jnp.minimum(cum[:, h : h + 1] - cum_t[h : h + 1, :], 0.0))
            b = beta[:, 4 + h : 5 + h]
            a = (kk * spread * b).astype(B16)
            r = (qk * spread).astype(B16)
            vb = (v_all[:, h * DV : (h + 1) * DV] * b).astype(B16)
            grow = growth[:, h : h + 1]
            src = jnp.concatenate([(kf * (b * grow)).astype(B16), vb], axis=1)
            fk = (kf * fade[:, h : h + 1]).astype(B16)
            terms.append([a, r, src, fk, qf * grow, growth[LEN - 1 : LEN, h : h + 1]])
    inv = [eye - t[0] * levels[0] for t in terms]
    for level in levels[1:]:
        part = [mm(t[0] * level, x).astype(B16) for t, x in zip(terms, inv)]
        inv = [x - mm(x, p).astype(B16) for x, p in zip(inv, part)]
    out = []
    for (a, r, src, fk, qg, last), x in zip(terms, inv):
        yw = mm(x, src).astype(B16)
        ryw = mm(r, yw)
        fyw = mm_tn(fk, yw)
        q_new = (qg - ryw[:, :DK]).astype(B16)
        out.append((q_new, ryw[:, DK:], fyw[:, :DK].astype(B16), fyw[:, DK:], last))
    return out


def local_kernel(pre_ref, tail_ref, gates_ref, taps_ref, par_ref, op_ref, os_ref, x_ref, ext):
    step = pl.program_id(0)
    rows = LEN * PER_STEP

    @pl.when(step == 0)
    def _():
        ext[0:8, :] = tail_ref[...].astype(F32)[8:16, :]
        eye = lax.broadcasted_iota(jnp.int32, (DK, 2 * DK), 0) == lax.broadcasted_iota(
            jnp.int32, (DK, 2 * DK), 1
        )
        for h in range(HEADS):
            x_ref[h] = eye.astype(F32)

    @pl.when(step > 0)
    def _():
        ext[0:8, :] = ext[rows : rows + 8, :]

    ext[8 : rows + 8, :] = pre_ref[...].astype(F32)
    taps = taps_ref[...]
    par = par_ref[...]
    done = []
    for c in range(PER_STEP):
        base = c * LEN + 8
        conv = taps[0:1, :] * ext[base - 3 : base - 3 + LEN, :]
        for j in range(1, KW):
            conv = conv + taps[j : j + 1, :] * ext[base - 3 + j : base - 3 + j + LEN, :]
        conv = silu(conv)
        done.append(
            chunk_terms(
                conv[:, :256], conv[:, 256:512], conv[:, 512:], gates_ref[c * LEN : (c + 1) * LEN, :], par
            )
        )
    for h in range(HEADS):
        x = x_ref[h]
        for c in range(PER_STEP):
            q_new, own, move, add, last = done[c][h]
            xb = x.astype(B16)
            seen = mm(q_new, xb)
            at = slice(c * LEN, (c + 1) * LEN)
            cols = slice(h * DV, (h + 1) * DV)
            op_ref[at, cols] = seen[:, :DK].astype(B16)
            os_ref[at, cols] = seen[:, DK:] + own
            x = x * last - mm(move, xb)
            x = jnp.concatenate([x[:, :DK], x[:, DK:] + add], axis=1)
        x_ref[h] = x


def local_pass(pre, tail, gates, taps, par):
    rows = LEN * PER_STEP
    total = pre.shape[0]
    return pl.pallas_call(
        local_kernel,
        grid=(total // rows,),
        in_specs=[
            pl.BlockSpec((rows, 1024), lambda i: (i, 0)),
            pl.BlockSpec((16, 1024), lambda i: (0, 0)),
            pl.BlockSpec((rows, 128), lambda i: (i, 0)),
            pl.BlockSpec((8, 1024), lambda i: (0, 0)),
            pl.BlockSpec((8, 128), lambda i: (0, 0)),
        ],
        out_specs=[
            pl.BlockSpec((rows, 512), lambda i: (i, 0)),
            pl.BlockSpec((rows, 512), lambda i: (i, 0)),
            pl.BlockSpec((HEADS, DK, 2 * DK), lambda i: (0, 0, 0)),
        ],
        out_shape=[
            jax.ShapeDtypeStruct((total, 512), B16),
            jax.ShapeDtypeStruct((total, 512), F32),
            jax.ShapeDtypeStruct((HEADS, DK, 2 * DK), F32),
        ],
        scratch_shapes=[pltpu.VMEM((rows + 8, 1024), F32)],
        compiler_params=pltpu.CompilerParams(
            dimension_semantics=("arbitrary",), vmem_limit_bytes=48 * 1024 * 1024
        ),
    )(pre, tail, gates, taps, par)


def finish_rows(seen, own, z, gain, state):
    parts = []
    for h in range(HEADS):
        cols = slice(h * DV, (h + 1) * DV)
        core = mm(seen[:, cols], state[h]) + own[:, cols]
        scale = lax.rsqrt(jnp.mean(core * core, axis=-1, keepdims=True) + EPSILON)
        parts.append((core * scale * gain * silu(z[:, cols].astype(F32))).astype(B16))
    return jnp.concatenate(parts, axis=1)


def finish_kernel(op_ref, os_ref, z_ref, gain_ref, state_ref, w_ref, out_ref):
    normed = finish_rows(op_ref[...], os_ref[...], z_ref[...], gain_ref[...], state_ref[...])
    out_ref[...] = mm(normed, w_ref[...]).astype(B16)


def finish(op, os, z, gain, state, w_out):
    rows = 160
    total, width = op.shape[0], w_out.shape[1]
    return pl.pallas_call(
        finish_kernel,
        grid=(total // rows,),
        in_specs=[
            pl.BlockSpec((rows, 512), lambda i: (i, 0)),
            pl.BlockSpec((rows, 512), lambda i: (i, 0)),
            pl.BlockSpec((rows, 512), lambda i: (i, 0)),
            pl.BlockSpec((1, DV), lambda i: (0, 0)),
            pl.BlockSpec((HEADS, DK, DV), lambda i: (0, 0, 0)),
            pl.BlockSpec((512, width), lambda i: (0, 0)),
        ],
        out_specs=pl.BlockSpec((rows, width), lambda i: (i, 0)),
        out_shape=jax.ShapeDtypeStruct((total, width), B16),
        compiler_params=pltpu.CompilerParams(
            dimension_semantics=("arbitrary",), vmem_limit_bytes=48 * 1024 * 1024
        ),
    )(op, os, z, gain, state, w_out)


def from_behind(block, axis, distance):
    devices = range(lax.axis_size(axis))
    route = [(i - distance, i) for i in devices if i - distance in devices]
    return lax.ppermute(block, axis, route)


def entering_state(x):
    x = from_behind(x.astype(B16), "context", 1)
    distance, count = 1, lax.axis_size("context")
    while distance < count:
        last = 2 * distance >= count
        sent = x[:, :, DK:] if last else x
        got = from_behind(sent, "context", distance)
        moved = jnp.einsum("hij,hjk->hik", x[:, :, :DK], got, preferred_element_type=F32)
        if last:
            x = moved + x[:, :, DK:].astype(F32)
        else:
            add = jnp.concatenate([jnp.zeros_like(x[:, :, :DK]), x[:, :, DK:]], axis=2)
            x = (moved + add.astype(F32)).astype(B16)
        distance *= 2
    return x.astype(B16)


def gate_weights(w_gates):
    order = w_gates.transpose(0, 2, 1).reshape(w_gates.shape[0], 2 * HEADS)
    return jnp.pad(order, ((0, 0), (0, 128 - 2 * HEADS)))


def small_inputs(conv_query, conv_key, conv_value, a_log, dt_bias, norm_gain):
    taps = jnp.concatenate([conv_query, conv_key, conv_value], axis=1).astype(F32)
    taps = jnp.pad(taps, ((0, 8 - KW), (0, 0)))
    par = jnp.pad(jnp.stack([a_log, dt_bias]), ((0, 6), (0, 128 - HEADS)))
    return taps, par, norm_gain.astype(F32)[None, :]


def per_device(
    tokens,
    w_query,
    w_key,
    w_value,
    w_gate_z,
    w_gates,
    conv_query,
    conv_key,
    conv_value,
    a_log,
    dt_bias,
    norm_gain,
    w_out,
):
    taps, par, gain = small_inputs(conv_query, conv_key, conv_value, a_log, dt_bias, norm_gain)
    gathered = lax.all_gather(tokens, "tensor", axis=0, tiled=True)
    weights = jnp.concatenate([w_query, w_key, w_value], axis=1)
    pre = mm(gathered, weights).astype(B16)
    tail = from_behind(pre[pre.shape[0] - 16 :], "context", 1)
    z = mm(gathered, w_gate_z).astype(B16)
    gates = mm(gathered, gate_weights(w_gates)).astype(B16)
    op, os, x = local_pass(pre, tail, gates, taps, par)
    state = entering_state(x)
    partial = finish(op, os, z, gain, state, w_out)
    return lax.psum_scatter(partial, "tensor", scatter_dimension=0, tiled=True)


def solution(mesh):
    placed = (
        P(("context", "tensor"), None),
        P(None, "tensor"),
        P(None, "tensor"),
        P(None, "tensor"),
        P(None, "tensor"),
        P(None, "tensor", None),
        P(None, "tensor"),
        P(None, "tensor"),
        P(None, "tensor"),
        P("tensor"),
        P("tensor"),
        P(),
        P("tensor", None),
    )
    return jax.shard_map(
        per_device,
        mesh=mesh,
        in_specs=placed,
        out_specs=P(("context", "tensor"), None),
        check_vma=False,
    )
```

```python
import functools

import jax
import jax.numpy as jnp
from jax import lax
from jax.experimental import pallas as pl
from jax.experimental.pallas import tpu as pltpu
from jax.sharding import PartitionSpec as P

HK = 16
HV = 32
DK = 128
DV = 128
KW = 4
EPSILON = 1e-06
LEN = 128
PER_STEP = 2
HEADS = 4
KEYS = 2
ROWS = 160
HALF = 80
F32 = jnp.float32
B16 = jnp.bfloat16


def mm(a, b):
    return jnp.dot(a, b, preferred_element_type=F32)


def mm_nt(a, b):
    return lax.dot_general(a, b, (((1,), (1,)), ((), ())), preferred_element_type=F32)


def mm_tn(a, b):
    return lax.dot_general(a, b, (((0,), (0,)), ((), ())), preferred_element_type=F32)


def silu(x):
    return x / (1.0 + jnp.exp(-x))


def unit(x):
    return x * lax.rsqrt(jnp.sum(x * x, axis=-1, keepdims=True) + EPSILON)


def chunk_terms(q_all, k_all, v_all, gates, gate_par):
    ii = lax.broadcasted_iota(jnp.int32, (LEN, LEN), 0)
    jj = lax.broadcasted_iota(jnp.int32, (LEN, LEN), 1)
    lower = (ii >= jj).astype(F32)
    strict = (ii > jj).astype(F32)
    differ = ii ^ jj
    levels = [((differ >> s) == 1).astype(B16) for s in range(LEN.bit_length() - 1)]
    eye = (ii == jj).astype(B16)

    logits = gates.astype(F32)
    shifted = logits + gate_par[1:2, :]
    softplus = jnp.maximum(shifted, 0.0) + jnp.log1p(jnp.exp(-jnp.abs(shifted)))
    decays = -jnp.exp(gate_par[0:1, :]) * softplus
    beta = 1.0 / (1.0 + jnp.exp(-logits))
    cum = jnp.dot(lower, decays, preferred_element_type=F32, precision=lax.Precision.HIGHEST)
    cum_t = cum.T
    growth = jnp.exp(cum)
    fade = jnp.exp(cum[LEN - 1 : LEN, :] - cum)

    terms = []
    for g in range(KEYS):
        qf = unit(q_all[:, g * DK : (g + 1) * DK]) * (DK**-0.5)
        kf = unit(k_all[:, g * DK : (g + 1) * DK])
        qb, kb = qf.astype(B16), kf.astype(B16)
        kk = mm_nt(kb, kb) * strict
        qk = mm_nt(qb, kb) * lower
        for h in (2 * g, 2 * g + 1):
            spread = jnp.exp(jnp.minimum(cum[:, h : h + 1] - cum_t[h : h + 1, :], 0.0))
            b = beta[:, 4 + h : 5 + h]
            a = (kk * spread * b).astype(B16)
            r = (qk * spread).astype(B16)
            vb = (v_all[:, h * DV : (h + 1) * DV] * b).astype(B16)
            grow = growth[:, h : h + 1]
            src = jnp.concatenate([(kf * (b * grow)).astype(B16), vb], axis=1)
            fk = (kf * fade[:, h : h + 1]).astype(B16)
            terms.append([a, r, src, fk, qf * grow, growth[LEN - 1 : LEN, h : h + 1]])
    inv = [eye - t[0] * levels[0] for t in terms]
    for level in levels[1:]:
        part = [mm(t[0] * level, x).astype(B16) for t, x in zip(terms, inv)]
        inv = [x - mm(x, p).astype(B16) for x, p in zip(inv, part)]
    out = []
    for (a, r, src, fk, qg, last), x in zip(terms, inv):
        yw = mm(x, src).astype(B16)
        ryw = mm(r, yw)
        fyw = mm_tn(fk, yw)
        q_new = (qg - ryw[:, :DK]).astype(B16)
        out.append((q_new, ryw[:, DK:], fyw[:, :DK].astype(B16), fyw[:, DK:], last))
    return out


def local_kernel(pre_ref, tail_ref, gates_ref, taps_ref, par_ref, op_ref, os_ref, x_ref, ext):
    step = pl.program_id(0)
    rows = LEN * PER_STEP

    @pl.when(step == 0)
    def _():
        ext[0:8, :] = tail_ref[...].astype(F32)[8:16, :]
        eye = lax.broadcasted_iota(jnp.int32, (DK, 2 * DK), 0) == lax.broadcasted_iota(
            jnp.int32, (DK, 2 * DK), 1
        )
        for h in range(HEADS):
            x_ref[h] = eye.astype(F32)

    @pl.when(step > 0)
    def _():
        ext[0:8, :] = ext[rows : rows + 8, :]

    ext[8 : rows + 8, :] = pre_ref[...].astype(F32)
    taps = taps_ref[...]
    par = par_ref[...]
    done = []
    for c in range(PER_STEP):
        base = c * LEN + 8
        conv = taps[0:1, :] * ext[base - 3 : base - 3 + LEN, :]
        for j in range(1, KW):
            conv = conv + taps[j : j + 1, :] * ext[base - 3 + j : base - 3 + j + LEN, :]
        conv = silu(conv)
        done.append(
            chunk_terms(
                conv[:, :256], conv[:, 256:512], conv[:, 512:], gates_ref[c * LEN : (c + 1) * LEN, :], par
            )
        )
    for h in range(HEADS):
        x = x_ref[h]
        for c in range(PER_STEP):
            q_new, own, move, add, last = done[c][h]
            xb = x.astype(B16)
            seen = mm(q_new, xb)
            at = slice(c * LEN, (c + 1) * LEN)
            cols = slice(h * DV, (h + 1) * DV)
            op_ref[at, cols] = seen[:, :DK].astype(B16)
            os_ref[at, cols] = seen[:, DK:] + own
            x = x * last - mm(move, xb)
            x = jnp.concatenate([x[:, :DK], x[:, DK:] + add], axis=1)
        x_ref[h] = x


def local_pass(pre, tail, gates, taps, par):
    rows = LEN * PER_STEP
    total = pre.shape[0]
    return pl.pallas_call(
        local_kernel,
        grid=(total // rows,),
        in_specs=[
            pl.BlockSpec((rows, 1024), lambda i: (i, 0)),
            pl.BlockSpec((16, 1024), lambda i: (0, 0)),
            pl.BlockSpec((rows, 128), lambda i: (i, 0)),
            pl.BlockSpec((8, 1024), lambda i: (0, 0)),
            pl.BlockSpec((8, 128), lambda i: (0, 0)),
        ],
        out_specs=[
            pl.BlockSpec((rows, 512), lambda i: (i, 0)),
            pl.BlockSpec((rows, 512), lambda i: (i, 0)),
            pl.BlockSpec((HEADS, DK, 2 * DK), lambda i: (0, 0, 0)),
        ],
        out_shape=[
            jax.ShapeDtypeStruct((total, 512), B16),
            jax.ShapeDtypeStruct((total, 512), F32),
            jax.ShapeDtypeStruct((HEADS, DK, 2 * DK), F32),
        ],
        scratch_shapes=[pltpu.VMEM((rows + 8, 1024), F32)],
        compiler_params=pltpu.CompilerParams(
            dimension_semantics=("arbitrary",), vmem_limit_bytes=48 * 1024 * 1024
        ),
    )(pre, tail, gates, taps, par)


def finish_rows(seen, own, z, gain, state):
    parts = []
    for h in range(HEADS):
        cols = slice(h * DV, (h + 1) * DV)
        core = mm(seen[:, cols], state[h]) + own[:, cols]
        scale = lax.rsqrt(jnp.mean(core * core, axis=-1, keepdims=True) + EPSILON)
        parts.append((core * scale * gain * silu(z[:, cols].astype(F32))).astype(B16))
    return jnp.concatenate(parts, axis=1)


def neighbours():
    me = lax.axis_index("tensor")
    y, x = me // 2, me % 2
    up, down, far = ((y + d) % 4 * 2 + x for d in (1, 3, 2))
    return me, up, down, far


def across(index):
    return index // 2 * 2 + 1 - index % 2


def greet(axis, partners):
    barrier = pltpu.get_barrier_semaphore()
    for partner in partners:
        pl.semaphore_signal(
            barrier, inc=1, device_id={axis: partner}, device_id_type=pl.DeviceIdType.MESH
        )
    pl.semaphore_wait(barrier, len(partners))


def rows_at(index, half=None):
    if half is None:
        return pl.ds(pl.multiple_of(index * ROWS, 16), ROWS)
    return pl.ds(pl.multiple_of(index * ROWS + half * HALF, 16), HALF)


def gather_kernel(
    tok_ref, wq_ref, wk_ref, wv_ref, wz_ref, wg_ref, pre_ref, z_ref, gates_ref,
    held, w_pre, w_z, w_g, w_sem, send_sem, recv_sem,
):
    me, up, down, far = neighbours()
    loads = [
        pltpu.make_async_copy(src, dst, w_sem.at[i])
        for i, (src, dst) in enumerate(
            (
                (wq_ref, w_pre.at[:, 0:256]),
                (wk_ref, w_pre.at[:, 256:512]),
                (wv_ref, w_pre.at[:, 512:1024]),
                (wz_ref, w_z),
                (wg_ref, w_g),
            )
        )
    ]
    for load in loads:
        load.start()
    greet("tensor", (up, down, across(me)))

    def copy(k, slot, half, target, own=False):
        return pltpu.make_async_remote_copy(
            src_ref=tok_ref.at[half * HALF : half * HALF + HALF] if own else held.at[rows_at(slot, half)],
            dst_ref=held.at[rows_at(slot, half)],
            send_sem=send_sem.at[k],
            recv_sem=recv_sem.at[k],
            device_id={"tensor": target},
            device_id_type=pl.DeviceIdType.MESH,
        )

    sent = []

    def send(k, slot, half, target, own=False):
        made = copy(k, slot, half, target, own)
        made.start()
        sent.append(made)

    def arrived(k, slot, half):
        copy(k, slot, half, me).wait_recv()

    def project(slot, own=False):
        source = tok_ref if own else held.at[rows_at(slot)]
        at = rows_at(slot)

        @pl.loop(0, 4)
        def _(i):
            cols = pl.ds(pl.multiple_of(i * 256, 256), 256)
            pre_ref[at, cols] = mm(source[...], w_pre[:, cols]).astype(B16)

        @pl.loop(0, 2)
        def _(i):
            cols = pl.ds(pl.multiple_of(i * 256, 256), 256)
            z_ref[at, cols] = mm(source[...], w_z[:, cols]).astype(B16)

        gates_ref[at, :] = mm(source[...], w_g[...]).astype(B16)

    send(0, me, 0, up, True)
    send(3, me, 1, down, True)
    send(4, me, 0, across(me), True)
    send(5, me, 1, across(me), True)
    send(1, me, 1, up, True)
    send(2, me, 0, down, True)
    for load in loads:
        load.wait()
    project(me, True)
    arrived(0, down, 0)
    send(6, down, 0, up)
    arrived(3, up, 1)
    send(7, up, 1, down)
    arrived(1, down, 1)
    project(down)
    arrived(2, up, 0)
    project(up)
    arrived(4, across(me), 0)
    send(8, across(me), 0, up)
    send(10, across(me), 0, down)
    arrived(5, across(me), 1)
    send(11, across(me), 1, down)
    send(9, across(me), 1, up)
    project(across(me))
    arrived(6, far, 0)
    arrived(7, far, 1)
    project(far)
    arrived(8, across(down), 0)
    send(12, across(down), 0, up)
    arrived(11, across(up), 1)
    send(13, across(up), 1, down)
    arrived(9, across(down), 1)
    project(across(down))
    arrived(10, across(up), 0)
    project(across(up))
    arrived(12, across(far), 0)
    arrived(13, across(far), 1)
    project(across(far))
    for made in sent:
        made.wait_send()


def gather_project(tokens, w_query, w_key, w_value, w_gate_z, w_gates):
    total, depth = 8 * ROWS, tokens.shape[1]
    vmem = pl.BlockSpec(memory_space=pltpu.VMEM)
    hbm = pl.BlockSpec(memory_space=pl.ANY)
    return pl.pallas_call(
        gather_kernel,
        in_specs=[vmem] + [hbm] * 5,
        out_specs=[vmem] * 3,
        out_shape=[
            jax.ShapeDtypeStruct((total, 1024), B16),
            jax.ShapeDtypeStruct((total, 512), B16),
            jax.ShapeDtypeStruct((total, 128), B16),
        ],
        scratch_shapes=[
            pltpu.VMEM((total, depth), B16),
            pltpu.VMEM((depth, 1024), B16),
            pltpu.VMEM((depth, 512), B16),
            pltpu.VMEM((depth, 128), B16),
            pltpu.SemaphoreType.DMA((5,)),
            pltpu.SemaphoreType.DMA((14,)),
            pltpu.SemaphoreType.DMA((14,)),
        ],
        compiler_params=pltpu.CompilerParams(
            collective_id=0, has_side_effects=True, vmem_limit_bytes=48 * 1024 * 1024
        ),
    )(tokens, w_query, w_key, w_value, w_gate_z, w_gates)


def finish_kernel(
    op_ref, os_ref, z_ref, gain_ref, state_ref, w_ref, out_ref,
    near, via, mine, got_via, got_up, got_down, got_x, send_sem, recv_sem,
):
    me, up, down, far = neighbours()
    greet("tensor", (up, down, across(me)))
    width = out_ref.shape[1]

    def share(index, g, store):
        row = across(index) if g == 0 else index
        at = rows_at(row)
        normed = finish_rows(op_ref[at, :], os_ref[at, :], z_ref[at, :], gain_ref[...], state_ref)

        @pl.loop(0, width // 512)
        def _(i):
            cols = pl.ds(pl.multiple_of(i * 512, 512), 512)
            store[:, cols] = mm(normed, w_ref[:, cols]).astype(B16)

    sent = []

    def copy(k, src, dst, target):
        return pltpu.make_async_remote_copy(
            src_ref=src,
            dst_ref=dst,
            send_sem=send_sem.at[k],
            recv_sem=recv_sem.at[k],
            device_id={"tensor": target},
            device_id_type=pl.DeviceIdType.MESH,
        )

    def send(k, src, dst, target):
        made = copy(k, src, dst, target)
        made.start()
        sent.append(made)

    def arrived(k, dst):
        copy(k, dst, dst, me).wait_recv()

    halves = (slice(0, HALF), slice(HALF, ROWS))

    def send_via(g):
        send(g * 6, via.at[g, halves[0]], got_via.at[g, halves[0]], up)
        send(g * 6 + 1, via.at[g, halves[1]], got_via.at[g, halves[1]], down)

    def send_up(g, half):
        send(g * 6 + 2 + half, near.at[g, 0, halves[half]], got_down.at[g, halves[half]], up)

    def send_down(g, half):
        send(g * 6 + 4 + half, near.at[g, 1, halves[half]], got_up.at[g, halves[half]], down)

    def relay(g):
        for way in (0, 1):
            arrived(g * 6 + way, got_via.at[g, halves[way]])
            near[g, way, halves[way], :] = (
                near[g, way, halves[way], :].astype(F32) + got_via[g, halves[way], :].astype(F32)
            ).astype(B16)
            (send_up, send_down)[way](g, way)

    def total(g, half):
        arrived(g * 6 + 2 + half, got_down.at[g, halves[half]])
        arrived(g * 6 + 4 + half, got_up.at[g, halves[half]])
        rows = halves[half]
        return (
            mine[g, rows, :].astype(F32) + got_down[g, rows, :].astype(F32) + got_up[g, rows, :].astype(F32)
        )

    share(far, 0, via.at[0])
    send_via(0)
    share(up, 0, near.at[0, 0])
    send_up(0, 1)
    share(down, 0, near.at[0, 1])
    send_down(0, 0)
    share(far, 1, via.at[1])
    share(up, 1, near.at[1, 0])
    share(down, 1, near.at[1, 1])
    relay(0)
    send_via(1)
    send_up(1, 1)
    send_down(1, 0)
    share(me, 0, mine.at[0])
    share(me, 1, mine.at[1])
    for half in (1, 0):
        mine[0, halves[half], :] = total(0, half).astype(B16)
        send(12 + half, mine.at[0, halves[half]], got_x.at[halves[half]], across(me))
    relay(1)
    for half in (1, 0):
        summed = total(1, half)
        arrived(12 + half, got_x.at[halves[half]])
        out_ref[halves[half], :] = (summed + got_x[halves[half], :].astype(F32)).astype(B16)
    for made in sent:
        made.wait_send()


def finish(op, os, z, gain, state, w_out):
    width = w_out.shape[1]
    vmem = pl.BlockSpec(memory_space=pltpu.VMEM)
    block = (ROWS, width)
    return pl.pallas_call(
        finish_kernel,
        in_specs=[vmem] * 6,
        out_specs=vmem,
        out_shape=jax.ShapeDtypeStruct(block, B16),
        scratch_shapes=[
            pltpu.VMEM((2, 2) + block, B16),
            pltpu.VMEM((2,) + block, B16),
            pltpu.VMEM((2,) + block, B16),
            pltpu.VMEM((2,) + block, B16),
            pltpu.VMEM((2,) + block, B16),
            pltpu.VMEM((2,) + block, B16),
            pltpu.VMEM(block, B16),
            pltpu.SemaphoreType.DMA((14,)),
            pltpu.SemaphoreType.DMA((14,)),
        ],
        compiler_params=pltpu.CompilerParams(
            collective_id=1, has_side_effects=True, vmem_limit_bytes=48 * 1024 * 1024
        ),
    )(op, os, z, gain, state, w_out)


def from_behind(block, axis, distance):
    devices = range(lax.axis_size(axis))
    route = [(i - distance, i) for i in devices if i - distance in devices]
    return lax.ppermute(block, axis, route)


def entering_state(x):
    x = from_behind(x.astype(B16), "context", 1)
    distance, count = 1, lax.axis_size("context")
    while distance < count:
        last = 2 * distance >= count
        sent = x[:, :, DK:] if last else x
        got = from_behind(sent, "context", distance)
        moved = jnp.einsum("hij,hjk->hik", x[:, :, :DK], got, preferred_element_type=F32)
        if last:
            x = moved + x[:, :, DK:].astype(F32)
        else:
            add = jnp.concatenate([jnp.zeros_like(x[:, :, :DK]), x[:, :, DK:]], axis=2)
            x = (moved + add.astype(F32)).astype(B16)
        distance *= 2
    return x.astype(B16)


def gate_weights(w_gates):
    order = w_gates.transpose(0, 2, 1).reshape(w_gates.shape[0], 2 * HEADS)
    return jnp.pad(order, ((0, 0), (0, 128 - 2 * HEADS)))


def small_inputs(conv_query, conv_key, conv_value, a_log, dt_bias, norm_gain):
    taps = jnp.concatenate([conv_query, conv_key, conv_value], axis=1).astype(F32)
    taps = jnp.pad(taps, ((0, 8 - KW), (0, 0)))
    par = jnp.pad(jnp.stack([a_log, dt_bias]), ((0, 6), (0, 128 - HEADS)))
    return taps, par, norm_gain.astype(F32)[None, :]


def per_device(
    tokens,
    w_query,
    w_key,
    w_value,
    w_gate_z,
    w_gates,
    conv_query,
    conv_key,
    conv_value,
    a_log,
    dt_bias,
    norm_gain,
    w_out,
):
    taps, par, gain = small_inputs(conv_query, conv_key, conv_value, a_log, dt_bias, norm_gain)
    pre, z, gates = gather_project(
        tokens, w_query, w_key, w_value, w_gate_z, gate_weights(w_gates)
    )
    tail = from_behind(pre[pre.shape[0] - 16 :], "context", 1)
    op, os, x = local_pass(pre, tail, gates, taps, par)
    state = entering_state(x)
    return finish(op, os, z, gain, state, w_out)


def solution(mesh):
    placed = (
        P(("context", "tensor"), None),
        P(None, "tensor"),
        P(None, "tensor"),
        P(None, "tensor"),
        P(None, "tensor"),
        P(None, "tensor", None),
        P(None, "tensor"),
        P(None, "tensor"),
        P(None, "tensor"),
        P("tensor"),
        P("tensor"),
        P(),
        P("tensor", None),
    )
    return jax.shard_map(
        per_device,
        mesh=mesh,
        in_specs=placed,
        out_specs=P(("context", "tensor"), None),
        check_vma=False,
    )
```

```python
import functools

import jax
import jax.numpy as jnp
from jax import lax
from jax.experimental import pallas as pl
from jax.experimental.pallas import tpu as pltpu
from jax.sharding import PartitionSpec as P

HK = 16
HV = 32
DK = 128
DV = 128
KW = 4
EPSILON = 1e-06
LEN = 128
PER_STEP = 2
HEADS = 4
KEYS = 2
ROWS = 160
HALF = 80
F32 = jnp.float32
B16 = jnp.bfloat16


def mm(a, b):
    return jnp.dot(a, b, preferred_element_type=F32)


def mm_nt(a, b):
    return lax.dot_general(a, b, (((1,), (1,)), ((), ())), preferred_element_type=F32)


def mm_tn(a, b):
    return lax.dot_general(a, b, (((0,), (0,)), ((), ())), preferred_element_type=F32)


def silu(x):
    return x / (1.0 + jnp.exp(-x))


def unit(x):
    return x * lax.rsqrt(jnp.sum(x * x, axis=-1, keepdims=True) + EPSILON)


def chunk_terms(q_all, k_all, v_all, gates, gate_par):
    ii = lax.broadcasted_iota(jnp.int32, (LEN, LEN), 0)
    jj = lax.broadcasted_iota(jnp.int32, (LEN, LEN), 1)
    lower = (ii >= jj).astype(F32)
    strict = (ii > jj).astype(F32)
    differ = ii ^ jj
    levels = [((differ >> s) == 1).astype(B16) for s in range(LEN.bit_length() - 1)]
    eye = (ii == jj).astype(B16)

    logits = gates.astype(F32)
    shifted = logits + gate_par[1:2, :]
    softplus = jnp.maximum(shifted, 0.0) + jnp.log1p(jnp.exp(-jnp.abs(shifted)))
    decays = -jnp.exp(gate_par[0:1, :]) * softplus
    beta = 1.0 / (1.0 + jnp.exp(-logits))
    cum = jnp.dot(lower, decays, preferred_element_type=F32, precision=lax.Precision.HIGHEST)
    cum_t = cum.T
    growth = jnp.exp(cum)
    fade = jnp.exp(cum[LEN - 1 : LEN, :] - cum)

    terms = []
    for g in range(KEYS):
        qf = unit(q_all[:, g * DK : (g + 1) * DK]) * (DK**-0.5)
        kf = unit(k_all[:, g * DK : (g + 1) * DK])
        qb, kb = qf.astype(B16), kf.astype(B16)
        kk = mm_nt(kb, kb) * strict
        qk = mm_nt(qb, kb) * lower
        for h in (2 * g, 2 * g + 1):
            spread = jnp.exp(jnp.minimum(cum[:, h : h + 1] - cum_t[h : h + 1, :], 0.0))
            b = beta[:, 4 + h : 5 + h]
            a = (kk * spread * b).astype(B16)
            r = (qk * spread).astype(B16)
            vb = (v_all[:, h * DV : (h + 1) * DV] * b).astype(B16)
            grow = growth[:, h : h + 1]
            src = jnp.concatenate([(kf * (b * grow)).astype(B16), vb], axis=1)
            fk = (kf * fade[:, h : h + 1]).astype(B16)
            terms.append([a, r, src, fk, qf * grow, growth[LEN - 1 : LEN, h : h + 1]])
    inv = [eye - t[0] * levels[0] for t in terms]
    for level in levels[1:]:
        part = [mm(t[0] * level, x).astype(B16) for t, x in zip(terms, inv)]
        inv = [x - mm(x, p).astype(B16) for x, p in zip(inv, part)]
    out = []
    for (a, r, src, fk, qg, last), x in zip(terms, inv):
        yw = mm(x, src).astype(B16)
        ryw = mm(r, yw)
        fyw = mm_tn(fk, yw)
        q_new = (qg - ryw[:, :DK]).astype(B16)
        out.append((q_new, ryw[:, DK:], fyw[:, :DK].astype(B16), fyw[:, DK:], last))
    return out


def local_kernel(pre_ref, tail_ref, gates_ref, taps_ref, par_ref, op_ref, os_ref, x_ref, ext):
    step = pl.program_id(0)
    rows = LEN * PER_STEP

    @pl.when(step == 0)
    def _():
        ext[0:8, :] = tail_ref[...].astype(F32)[8:16, :]
        eye = lax.broadcasted_iota(jnp.int32, (DK, 2 * DK), 0) == lax.broadcasted_iota(
            jnp.int32, (DK, 2 * DK), 1
        )
        for h in range(HEADS):
            x_ref[h] = eye.astype(F32)

    @pl.when(step > 0)
    def _():
        ext[0:8, :] = ext[rows : rows + 8, :]

    ext[8 : rows + 8, :] = pre_ref[...].astype(F32)
    taps = taps_ref[...]
    par = par_ref[...]
    done = []
    for c in range(PER_STEP):
        base = c * LEN + 8
        conv = taps[0:1, :] * ext[base - 3 : base - 3 + LEN, :]
        for j in range(1, KW):
            conv = conv + taps[j : j + 1, :] * ext[base - 3 + j : base - 3 + j + LEN, :]
        conv = silu(conv)
        done.append(
            chunk_terms(
                conv[:, :256], conv[:, 256:512], conv[:, 512:], gates_ref[c * LEN : (c + 1) * LEN, :], par
            )
        )
    for h in range(HEADS):
        x = x_ref[h]
        for c in range(PER_STEP):
            q_new, own, move, add, last = done[c][h]
            xb = x.astype(B16)
            seen = mm(q_new, xb)
            at = slice(c * LEN, (c + 1) * LEN)
            cols = slice(h * DV, (h + 1) * DV)
            op_ref[at, cols] = seen[:, :DK].astype(B16)
            os_ref[at, cols] = seen[:, DK:] + own
            x = x * last - mm(move, xb)
            x = jnp.concatenate([x[:, :DK], x[:, DK:] + add], axis=1)
        x_ref[h] = x


def local_pass(pre, tail, gates, taps, par):
    rows = LEN * PER_STEP
    total = pre.shape[0]
    return pl.pallas_call(
        local_kernel,
        grid=(total // rows,),
        in_specs=[
            pl.BlockSpec((rows, 1024), lambda i: (i, 0)),
            pl.BlockSpec((16, 1024), lambda i: (0, 0)),
            pl.BlockSpec((rows, 128), lambda i: (i, 0)),
            pl.BlockSpec((8, 1024), lambda i: (0, 0)),
            pl.BlockSpec((8, 128), lambda i: (0, 0)),
        ],
        out_specs=[
            pl.BlockSpec((rows, 512), lambda i: (i, 0)),
            pl.BlockSpec((rows, 512), lambda i: (i, 0)),
            pl.BlockSpec((HEADS, DK, 2 * DK), lambda i: (0, 0, 0)),
        ],
        out_shape=[
            jax.ShapeDtypeStruct((total, 512), B16),
            jax.ShapeDtypeStruct((total, 512), F32),
            jax.ShapeDtypeStruct((HEADS, DK, 2 * DK), F32),
        ],
        scratch_shapes=[pltpu.VMEM((rows + 8, 1024), F32)],
        compiler_params=pltpu.CompilerParams(
            dimension_semantics=("arbitrary",), vmem_limit_bytes=48 * 1024 * 1024
        ),
    )(pre, tail, gates, taps, par)


def finish_rows(seen, own, z, gain, state):
    parts = []
    for h in range(HEADS):
        cols = slice(h * DV, (h + 1) * DV)
        core = mm(seen[:, cols], state[h]) + own[:, cols]
        scale = lax.rsqrt(jnp.mean(core * core, axis=-1, keepdims=True) + EPSILON)
        parts.append((core * scale * gain * silu(z[:, cols].astype(F32))).astype(B16))
    return jnp.concatenate(parts, axis=1)


def neighbours():
    me = lax.axis_index("tensor")
    y, x = me // 2, me % 2
    up, down, far = ((y + d) % 4 * 2 + x for d in (1, 3, 2))
    return me, up, down, far


def across(index):
    return index // 2 * 2 + 1 - index % 2


def greet(axis, partners):
    barrier = pltpu.get_barrier_semaphore()
    for partner in partners:
        pl.semaphore_signal(
            barrier, inc=1, device_id={axis: partner}, device_id_type=pl.DeviceIdType.MESH
        )
    pl.semaphore_wait(barrier, len(partners))


def rows_at(index, half=None):
    if half is None:
        return pl.ds(pl.multiple_of(index * ROWS, 16), ROWS)
    return pl.ds(pl.multiple_of(index * ROWS + half * HALF, 16), HALF)


def gather_kernel(
    tok_ref, wq_ref, wk_ref, wv_ref, wz_ref, wg_ref, pre_ref, z_ref, gates_ref,
    held, w_pre, w_z, w_g, w_sem, send_sem, recv_sem,
):
    me, up, down, far = neighbours()
    loads = [
        pltpu.make_async_copy(src, dst, w_sem.at[i])
        for i, (src, dst) in enumerate(
            (
                (wq_ref, w_pre.at[:, 0:256]),
                (wk_ref, w_pre.at[:, 256:512]),
                (wv_ref, w_pre.at[:, 512:1024]),
                (wz_ref, w_z),
                (wg_ref, w_g),
            )
        )
    ]
    for load in loads:
        load.start()
    greet("tensor", (up, down, across(me)))

    def copy(k, slot, half, target, own=False):
        return pltpu.make_async_remote_copy(
            src_ref=tok_ref.at[half * HALF : half * HALF + HALF] if own else held.at[rows_at(slot, half)],
            dst_ref=held.at[rows_at(slot, half)],
            send_sem=send_sem.at[k],
            recv_sem=recv_sem.at[k],
            device_id={"tensor": target},
            device_id_type=pl.DeviceIdType.MESH,
        )

    sent = []

    def send(k, slot, half, target, own=False):
        made = copy(k, slot, half, target, own)
        made.start()
        sent.append(made)

    def arrived(k, slot, half):
        copy(k, slot, half, me).wait_recv()

    def project(slot, own=False):
        source = tok_ref if own else held.at[rows_at(slot)]
        at = rows_at(slot)

        @pl.loop(0, 4)
        def _(i):
            cols = pl.ds(pl.multiple_of(i * 256, 256), 256)
            pre_ref[at, cols] = mm(source[...], w_pre[:, cols]).astype(B16)

        @pl.loop(0, 2)
        def _(i):
            cols = pl.ds(pl.multiple_of(i * 256, 256), 256)
            z_ref[at, cols] = mm(source[...], w_z[:, cols]).astype(B16)

        gates_ref[at, :] = mm(source[...], w_g[...]).astype(B16)

    beside, beside_down, beside_up, beside_far = (across(i) for i in (me, down, up, far))
    send(0, me, 1, up, True)
    send(2, me, 0, down, True)
    send(4, me, 0, beside, True)
    send(5, me, 1, beside, True)
    send(1, me, 0, up, True)
    send(3, me, 1, down, True)
    for load in loads:
        load.wait()
    project(me, True)
    arrived(0, down, 1)
    send(6, down, 1, beside)
    arrived(2, up, 0)
    send(7, up, 0, beside)
    arrived(4, beside, 0)
    send(10, beside, 0, up)
    arrived(1, down, 0)
    send(8, down, 0, up)
    arrived(3, up, 1)
    send(9, up, 1, down)
    arrived(5, beside, 1)
    send(11, beside, 1, down)
    project(down)
    project(up)
    project(beside)
    arrived(10, beside_down, 0)
    send(12, beside_down, 0, up)
    arrived(11, beside_up, 1)
    send(13, beside_up, 1, down)
    arrived(8, far, 0)
    arrived(9, far, 1)
    project(far)
    arrived(6, beside_down, 1)
    project(beside_down)
    arrived(7, beside_up, 0)
    project(beside_up)
    arrived(12, beside_far, 0)
    arrived(13, beside_far, 1)
    project(beside_far)
    for made in sent:
        made.wait_send()


def gather_project(tokens, w_query, w_key, w_value, w_gate_z, w_gates):
    total, depth = 8 * ROWS, tokens.shape[1]
    vmem = pl.BlockSpec(memory_space=pltpu.VMEM)
    hbm = pl.BlockSpec(memory_space=pl.ANY)
    return pl.pallas_call(
        gather_kernel,
        in_specs=[vmem] + [hbm] * 5,
        out_specs=[vmem] * 3,
        out_shape=[
            jax.ShapeDtypeStruct((total, 1024), B16),
            jax.ShapeDtypeStruct((total, 512), B16),
            jax.ShapeDtypeStruct((total, 128), B16),
        ],
        scratch_shapes=[
            pltpu.VMEM((total, depth), B16),
            pltpu.VMEM((depth, 1024), B16),
            pltpu.VMEM((depth, 512), B16),
            pltpu.VMEM((depth, 128), B16),
            pltpu.SemaphoreType.DMA((5,)),
            pltpu.SemaphoreType.DMA((14,)),
            pltpu.SemaphoreType.DMA((14,)),
        ],
        compiler_params=pltpu.CompilerParams(
            collective_id=0, has_side_effects=True, vmem_limit_bytes=48 * 1024 * 1024
        ),
    )(tokens, w_query, w_key, w_value, w_gate_z, w_gates)


def finish_kernel(
    op_ref, os_ref, z_ref, gain_ref, state_ref, w_ref, out_ref, part, got, send_sem, recv_sem
):
    me, up, down, far = neighbours()
    beside = across(me)
    greet("tensor", (up, down, beside))
    width = out_ref.shape[1]

    def share(slot, row):
        at = rows_at(row)
        normed = finish_rows(op_ref[at, :], os_ref[at, :], z_ref[at, :], gain_ref[...], state_ref)

        @pl.loop(0, width // 512)
        def _(i):
            cols = pl.ds(pl.multiple_of(i * 512, 512), 512)
            part[slot, :, cols] = mm(normed, w_ref[:, cols]).astype(B16)

    halves = (slice(0, HALF), slice(HALF, ROWS))
    sent = []

    def copy(k, slot, into, half, target):
        return pltpu.make_async_remote_copy(
            src_ref=part.at[slot, halves[half]],
            dst_ref=got.at[into, halves[half]],
            send_sem=send_sem.at[k],
            recv_sem=recv_sem.at[k],
            device_id={"tensor": target},
            device_id_type=pl.DeviceIdType.MESH,
        )

    def send(k, slot, into, half, target):
        made = copy(k, slot, into, half, target)
        made.start()
        sent.append(made)

    def arrived(k, into, half):
        copy(k, 0, into, half, me).wait_recv()

    def add(k, slot, into, half):
        arrived(k, into, half)
        rows = halves[half]
        part[slot, rows, :] = (
            part[slot, rows, :].astype(F32) + got[into, rows, :].astype(F32)
        ).astype(B16)

    share(0, across(far))
    send(0, 0, 0, 0, down)
    send(1, 0, 0, 1, up)
    share(1, across(down))
    send(2, 1, 1, 1, beside)
    share(2, across(up))
    send(3, 2, 1, 0, beside)
    share(4, far)
    share(3, beside)
    add(0, 1, 0, 0)
    send(4, 1, 2, 0, down)
    add(1, 2, 0, 1)
    send(5, 2, 2, 1, up)
    share(5, down)
    share(6, up)
    share(7, me)
    send(8, 4, 4, 0, down)
    send(9, 4, 4, 1, up)
    add(4, 3, 2, 0)
    send(6, 3, 3, 0, beside)
    add(5, 3, 2, 1)
    send(7, 3, 3, 1, beside)
    add(2, 5, 1, 1)
    send(11, 5, 5, 1, down)
    add(3, 6, 1, 0)
    send(12, 6, 6, 0, up)
    add(8, 5, 4, 0)
    send(10, 5, 5, 0, down)
    add(9, 6, 4, 1)
    send(13, 6, 6, 1, up)
    for half, ks in ((0, (6, 12, 10)), (1, (7, 11, 13))):
        for k in ks:
            arrived(k, {6: 3, 7: 3, 10: 5, 11: 5, 12: 6, 13: 6}[k], half)
        rows = halves[half]
        total = part[7, rows, :].astype(F32)
        for into in (3, 5, 6):
            total = total + got[into, rows, :].astype(F32)
        out_ref[rows, :] = total.astype(B16)
    for made in sent:
        made.wait_send()


def finish(op, os, z, gain, state, w_out):
    width = w_out.shape[1]
    vmem = pl.BlockSpec(memory_space=pltpu.VMEM)
    return pl.pallas_call(
        finish_kernel,
        in_specs=[vmem] * 6,
        out_specs=vmem,
        out_shape=jax.ShapeDtypeStruct((ROWS, width), B16),
        scratch_shapes=[
            pltpu.VMEM((8, ROWS, width), B16),
            pltpu.VMEM((7, ROWS, width), B16),
            pltpu.SemaphoreType.DMA((14,)),
            pltpu.SemaphoreType.DMA((14,)),
        ],
        compiler_params=pltpu.CompilerParams(
            collective_id=1, has_side_effects=True, vmem_limit_bytes=48 * 1024 * 1024
        ),
    )(op, os, z, gain, state, w_out)


def from_behind(block, axis, distance):
    devices = range(lax.axis_size(axis))
    route = [(i - distance, i) for i in devices if i - distance in devices]
    return lax.ppermute(block, axis, route)


def scan_kernel(
    x_ref, state_ref, local, pair, ring, total, before, give, back, send_sem, recv_sem
):
    me = lax.axis_index("context")
    core, z, half = me % 2, me // 2 % 8, me // 16

    def at(new_z):
        return (half * 8 + (new_z + 8) % 8) * 2 + core

    above, below = at(z + 1), at(z - 1)
    other_core = me + 1 - 2 * core
    other_half = me + 16 - 32 * half
    greet("context", (above, below, other_core, other_half))
    mine, theirs = pl.ds(core * 2, 2), pl.ds(2 - core * 2, 2)

    def copy(k, src, dst, target):
        return pltpu.make_async_remote_copy(
            src_ref=src,
            dst_ref=dst,
            send_sem=send_sem.at[k],
            recv_sem=recv_sem.at[k],
            device_id={"context": target},
            device_id_type=pl.DeviceIdType.MESH,
        )

    local[...] = x_ref[...].astype(B16)
    swap = copy(0, local.at[theirs], pair, other_core)
    swap.start()
    swap.wait_recv()
    first_core = core == 0
    firsts = []
    sent = [swap]
    no_add = jnp.zeros((DK, DK), F32)

    def apply(second, first):
        added = jnp.concatenate([no_add, second[:, DK:].astype(F32)], axis=1)
        return mm(second[:, :DK], first) + added

    def slot(distance, i):
        return ring.at[(z + distance + 8) % 8, i]

    def send(k, distance, i, target):
        made = copy(k, slot(distance, i), slot(distance, i), target)
        made.start()
        sent.append(made)

    def arrived(k, distance, i):
        copy(k, slot(distance, i), slot(distance, i), other_core).wait_recv()

    for i in range(2):
        own, got = local[core * 2 + i].astype(F32), pair[i].astype(F32)
        first = jnp.where(first_core, own, got).astype(B16)
        second = jnp.where(first_core, got, own).astype(B16)
        firsts.append(first)
        ring[z, i] = apply(second, first).astype(B16)
        send(1 + i, 0, i, above)
        send(3 + i, 0, i, below)
    for step in (1, 2, 3):
        for i in range(2):
            arrived(4 * step - 3 + i, -step, i)
            arrived(4 * step - 1 + i, step, i)
            if step < 3 or i == 0:
                send(4 * step + 1 + i, -step, i, above)
            if step < 3 or i == 1:
                send(4 * step + 3 + i, step, i, below)
    arrived(13, 4, 0)
    arrived(16, 4, 1)
    folded = []
    for i in range(2):
        start = lax.broadcasted_iota(jnp.int32, (DK, 2 * DK), 0) == lax.broadcasted_iota(
            jnp.int32, (DK, 2 * DK), 1
        )
        run = start.astype(F32)
        here = run
        for chip in range(8):
            here = jnp.where(z == chip, run, here)
            run = apply(ring[chip, i], run.astype(B16))
        folded.append(here)
        total[i] = run[:, DK:].astype(B16)
    onward = copy(17, total, before, other_half)

    @pl.when(half == 0)
    def _():
        before[...] = jnp.zeros_like(before)
        onward.start()
        onward.wait_send()

    @pl.when(half == 1)
    def _():
        onward.wait_recv()

    for i in range(2):
        here = folded[i]
        entering = mm(here[:, :DK].astype(B16), before[i]) + here[:, DK:]
        first = firsts[i]
        later = mm(first[:, :DK], entering.astype(B16)) + first[:, DK:].astype(F32)
        state_ref[core * 2 + i] = jnp.where(first_core, entering, later).astype(B16)
        give[i] = jnp.where(first_core, later, entering).astype(B16)
    swap_back = copy(18, give, back, other_core)
    swap_back.start()
    swap_back.wait()
    for i in range(2):
        state_ref[2 - core * 2 + i] = back[i]
    for made in sent:
        made.wait_send()


def entering_state(x):
    vmem = pl.BlockSpec(memory_space=pltpu.VMEM)
    return pl.pallas_call(
        scan_kernel,
        in_specs=[vmem],
        out_specs=vmem,
        out_shape=jax.ShapeDtypeStruct((HEADS, DK, DV), B16),
        scratch_shapes=[
            pltpu.VMEM((HEADS, DK, 2 * DK), B16),
            pltpu.VMEM((2, DK, 2 * DK), B16),
            pltpu.VMEM((8, 2, DK, 2 * DK), B16),
            pltpu.VMEM((2, DK, DV), B16),
            pltpu.VMEM((2, DK, DV), B16),
            pltpu.VMEM((2, DK, DV), B16),
            pltpu.VMEM((2, DK, DV), B16),
            pltpu.SemaphoreType.DMA((19,)),
            pltpu.SemaphoreType.DMA((19,)),
        ],
        compiler_params=pltpu.CompilerParams(
            collective_id=2, has_side_effects=True, vmem_limit_bytes=48 * 1024 * 1024
        ),
    )(x)


def gate_weights(w_gates):
    order = w_gates.transpose(0, 2, 1).reshape(w_gates.shape[0], 2 * HEADS)
    return jnp.pad(order, ((0, 0), (0, 128 - 2 * HEADS)))


def small_inputs(conv_query, conv_key, conv_value, a_log, dt_bias, norm_gain):
    taps = jnp.concatenate([conv_query, conv_key, conv_value], axis=1).astype(F32)
    taps = jnp.pad(taps, ((0, 8 - KW), (0, 0)))
    par = jnp.pad(jnp.stack([a_log, dt_bias]), ((0, 6), (0, 128 - HEADS)))
    return taps, par, norm_gain.astype(F32)[None, :]


def per_device(
    tokens,
    w_query,
    w_key,
    w_value,
    w_gate_z,
    w_gates,
    conv_query,
    conv_key,
    conv_value,
    a_log,
    dt_bias,
    norm_gain,
    w_out,
):
    taps, par, gain = small_inputs(conv_query, conv_key, conv_value, a_log, dt_bias, norm_gain)
    pre, z, gates = gather_project(
        tokens, w_query, w_key, w_value, w_gate_z, gate_weights(w_gates)
    )
    tail = from_behind(pre[pre.shape[0] - 16 :], "context", 1)
    op, os, x = local_pass(pre, tail, gates, taps, par)
    state = entering_state(x)
    return finish(op, os, z, gain, state, w_out)


def solution(mesh):
    placed = (
        P(("context", "tensor"), None),
        P(None, "tensor"),
        P(None, "tensor"),
        P(None, "tensor"),
        P(None, "tensor"),
        P(None, "tensor", None),
        P(None, "tensor"),
        P(None, "tensor"),
        P(None, "tensor"),
        P("tensor"),
        P("tensor"),
        P(),
        P("tensor", None),
    )
    return jax.shard_map(
        per_device,
        mesh=mesh,
        in_specs=placed,
        out_specs=P(("context", "tensor"), None),
        check_vma=False,
    )
```

```python
import functools

import jax
import jax.numpy as jnp
from jax import lax
from jax.experimental import pallas as pl
from jax.experimental.pallas import tpu as pltpu
from jax.sharding import PartitionSpec as P

HK = 16
HV = 32
DK = 128
DV = 128
KW = 4
EPSILON = 1e-06
LEN = 128
PER_STEP = 5
SOLVE = 64
HEADS = 4
KEYS = 2
ROWS = 160
HALF = 80
F32 = jnp.float32
B16 = jnp.bfloat16


def mm(a, b):
    return jnp.dot(a, b, preferred_element_type=F32)


def mm_nt(a, b):
    return lax.dot_general(a, b, (((1,), (1,)), ((), ())), preferred_element_type=F32)


def mm_tn(a, b):
    return lax.dot_general(a, b, (((0,), (0,)), ((), ())), preferred_element_type=F32)


def silu(x):
    return x / (1.0 + jnp.exp(-x))


def unit(x):
    return x * lax.rsqrt(jnp.sum(x * x, axis=-1, keepdims=True) + EPSILON)


def chunk_terms(convs, gates, gate_par):
    ii = lax.broadcasted_iota(jnp.int32, (LEN, LEN), 0)
    jj = lax.broadcasted_iota(jnp.int32, (LEN, LEN), 1)
    lower = (ii >= jj).astype(F32)
    strict = (ii > jj).astype(F32)
    differ = ii ^ jj
    levels = [((differ >> s) == 1).astype(B16) for s in range(SOLVE.bit_length() - 1)]
    eye = (ii == jj).astype(B16)

    units = []
    for conv in convs:
        for g in range(KEYS):
            qf = unit(conv[:, g * DK : (g + 1) * DK]) * (DK**-0.5)
            kf = unit(conv[:, 256 + g * DK : 256 + (g + 1) * DK])
            units.append((qf, kf, qf.astype(B16), kf.astype(B16)))
    kks = [mm_nt(kb, kb) * strict for _, _, _, kb in units]
    qks = [mm_nt(qb, kb) * lower for _, _, qb, kb in units]

    logits = [gate.astype(F32) for gate in gates]
    shifted = [x + gate_par[1:2, :] for x in logits]
    softplus = [jnp.maximum(x, 0.0) + jnp.log1p(jnp.exp(-jnp.abs(x))) for x in shifted]
    rate = -jnp.exp(gate_par[0:1, :])
    cums = [
        jnp.dot(lower, rate * x, preferred_element_type=F32, precision=lax.Precision.HIGHEST)
        for x in softplus
    ]

    terms = []
    for c, (conv, cum) in enumerate(zip(convs, cums)):
        beta = 1.0 / (1.0 + jnp.exp(-logits[c]))
        cum_t = cum.T
        growth = jnp.exp(cum)
        fade = jnp.exp(cum[LEN - 1 : LEN, :] - cum)
        for h in range(HEADS):
            qf, kf, _, _ = units[c * KEYS + h // 2]
            kk, qk = kks[c * KEYS + h // 2], qks[c * KEYS + h // 2]
            spread = jnp.exp(jnp.minimum(cum[:, h : h + 1] - cum_t[h : h + 1, :], 0.0))
            b = beta[:, 4 + h : 5 + h]
            a = (kk * spread * b).astype(B16)
            r = (qk * spread).astype(B16)
            vb = (conv[:, 512 + h * DV : 512 + (h + 1) * DV] * b).astype(B16)
            grow = growth[:, h : h + 1]
            src = jnp.concatenate([(kf * (b * grow)).astype(B16), vb], axis=1)
            fk = (kf * fade[:, h : h + 1]).astype(B16)
            terms.append((a, r, src, fk, qf * grow, growth[LEN - 1 : LEN, h : h + 1]))
    inv = [eye - t[0] * levels[0] for t in terms]
    for level in levels[1:]:
        part = [mm(t[0] * level, x).astype(B16) for t, x in zip(terms, inv)]
        inv = [x - mm(x, p).astype(B16) for x, p in zip(inv, part)]
    found = [[] for _ in terms]
    for i in range(LEN // SOLVE):
        rows = slice(i * SOLVE, (i + 1) * SOLVE)
        rhs = [t[2][rows] for t in terms]
        if i:
            known = [jnp.concatenate(f, axis=0) if i > 1 else f[0] for f in found]
            rhs = [
                (x.astype(F32) - mm(t[0][rows, : i * SOLVE], k)).astype(B16)
                for t, x, k in zip(terms, rhs, known)
            ]
        for f, x, y in zip(found, inv, rhs):
            f.append(mm(x[rows, rows], y).astype(B16))
    yws = [jnp.concatenate(f, axis=0) for f in found]
    fyws = [mm_tn(t[3], yw) for t, yw in zip(terms, yws)]
    ryws = [mm(t[1], yw) for t, yw in zip(terms, yws)]
    return [
        ((t[4] - ryw[:, :DK]).astype(B16), ryw[:, DK:], fyw[:, :DK].astype(B16), fyw[:, DK:], t[5])
        for t, ryw, fyw in zip(terms, ryws, fyws)
    ]


def local_kernel(pre_ref, tail_ref, gates_ref, taps_ref, par_ref, op_ref, os_ref, x_ref, ext):
    step = pl.program_id(0)
    rows = LEN * PER_STEP

    @pl.when(step == 0)
    def _():
        ext[0:8, :] = tail_ref[...].astype(F32)[8:16, :]
        eye = lax.broadcasted_iota(jnp.int32, (DK, 2 * DK), 0) == lax.broadcasted_iota(
            jnp.int32, (DK, 2 * DK), 1
        )
        for h in range(HEADS):
            x_ref[h] = eye.astype(F32)

    @pl.when(step > 0)
    def _():
        ext[0:8, :] = ext[rows : rows + 8, :]

    ext[8 : rows + 8, :] = pre_ref[...].astype(F32)
    taps = taps_ref[...]
    par = par_ref[...]
    convs = []
    for c in range(PER_STEP):
        base = c * LEN + 8
        conv = taps[0:1, :] * ext[base - 3 : base - 3 + LEN, :]
        for j in range(1, KW):
            conv = conv + taps[j : j + 1, :] * ext[base - 3 + j : base - 3 + j + LEN, :]
        convs.append(silu(conv))
    gates = [gates_ref[c * LEN : (c + 1) * LEN, :] for c in range(PER_STEP)]
    done = chunk_terms(convs, gates, par)
    xs = [x_ref[h] for h in range(HEADS)]
    for c in range(PER_STEP):
        at = slice(c * LEN, (c + 1) * LEN)
        now = done[c * HEADS : (c + 1) * HEADS]
        xbs = [x.astype(B16) for x in xs]
        moved = [mm(d[2], xb) for d, xb in zip(now, xbs)]
        seen = [mm(d[0], xb) for d, xb in zip(now, xbs)]
        for h in range(HEADS):
            cols = slice(h * DV, (h + 1) * DV)
            op_ref[at, cols] = seen[h][:, :DK].astype(B16)
            os_ref[at, cols] = seen[h][:, DK:] + now[h][1]
            x = xs[h] * now[h][4] - moved[h]
            xs[h] = jnp.concatenate([x[:, :DK], x[:, DK:] + now[h][3]], axis=1)
    for h in range(HEADS):
        x_ref[h] = xs[h]


def local_pass(pre, tail, gates, taps, par):
    rows = LEN * PER_STEP
    total = pre.shape[0]
    return pl.pallas_call(
        local_kernel,
        grid=(total // rows,),
        in_specs=[
            pl.BlockSpec((rows, 1024), lambda i: (i, 0)),
            pl.BlockSpec((16, 1024), lambda i: (0, 0)),
            pl.BlockSpec((rows, 128), lambda i: (i, 0)),
            pl.BlockSpec((8, 1024), lambda i: (0, 0)),
            pl.BlockSpec((8, 128), lambda i: (0, 0)),
        ],
        out_specs=[
            pl.BlockSpec((rows, 512), lambda i: (i, 0)),
            pl.BlockSpec((rows, 512), lambda i: (i, 0)),
            pl.BlockSpec((HEADS, DK, 2 * DK), lambda i: (0, 0, 0)),
        ],
        out_shape=[
            jax.ShapeDtypeStruct((total, 512), B16),
            jax.ShapeDtypeStruct((total, 512), F32),
            jax.ShapeDtypeStruct((HEADS, DK, 2 * DK), F32),
        ],
        scratch_shapes=[pltpu.VMEM((rows + 8, 1024), F32)],
        compiler_params=pltpu.CompilerParams(
            dimension_semantics=("arbitrary",), vmem_limit_bytes=48 * 1024 * 1024
        ),
    )(pre, tail, gates, taps, par)


def finish_rows(seen, own, z, gain, state):
    parts = []
    for h in range(HEADS):
        cols = slice(h * DV, (h + 1) * DV)
        core = mm(seen[:, cols], state[h]) + own[:, cols]
        scale = lax.rsqrt(jnp.mean(core * core, axis=-1, keepdims=True) + EPSILON)
        parts.append((core * scale * gain * silu(z[:, cols].astype(F32))).astype(B16))
    return jnp.concatenate(parts, axis=1)


def neighbours():
    me = lax.axis_index("tensor")
    y, x = me // 2, me % 2
    up, down, far = ((y + d) % 4 * 2 + x for d in (1, 3, 2))
    return me, up, down, far


def across(index):
    return index // 2 * 2 + 1 - index % 2


def greet(partners):
    barrier = pltpu.get_barrier_semaphore()
    partners = tuple(partners)
    for partner in partners:
        pl.semaphore_signal(
            barrier, inc=1, device_id=partner, device_id_type=pl.DeviceIdType.MESH
        )
    pl.semaphore_wait(barrier, len(partners))


def rows_at(index, half=None):
    if half is None:
        return pl.ds(pl.multiple_of(index * ROWS, 16), ROWS)
    return pl.ds(pl.multiple_of(index * ROWS + half * HALF, 16), HALF)


def gather_kernel(
    tok_ref, wq_ref, wk_ref, wv_ref, wz_ref, wg_ref, pre_ref, z_ref, gates_ref, tail_ref,
    held, got_tail, w_pre, w_z, w_g, w_sem, send_sem, recv_sem,
):
    me, up, down, far = neighbours()
    loads = [
        pltpu.make_async_copy(src, dst, w_sem.at[i])
        for i, (src, dst) in enumerate(
            (
                (wq_ref, w_pre.at[:, 0:256]),
                (wk_ref, w_pre.at[:, 256:512]),
                (wv_ref, w_pre.at[:, 512:1024]),
                (wz_ref, w_z),
                (wg_ref, w_g),
            )
        )
    ]
    for load in loads:
        load.start()
    context = lax.axis_index("context")
    after = (context + 1) % 32
    greet(
        [{"tensor": i} for i in (up, down, across(me))]
        + [{"context": i} for i in (after, (context + 31) % 32)]
    )
    tail_copy = pltpu.make_async_remote_copy(
        src_ref=pre_ref.at[8 * ROWS - 16 : 8 * ROWS],
        dst_ref=got_tail,
        send_sem=send_sem.at[14],
        recv_sem=recv_sem.at[14],
        device_id={"context": after},
        device_id_type=pl.DeviceIdType.MESH,
    )

    def copy(k, slot, half, target, own=False):
        return pltpu.make_async_remote_copy(
            src_ref=tok_ref.at[half * HALF : half * HALF + HALF] if own else held.at[rows_at(slot, half)],
            dst_ref=held.at[rows_at(slot, half)],
            send_sem=send_sem.at[k],
            recv_sem=recv_sem.at[k],
            device_id={"tensor": target},
            device_id_type=pl.DeviceIdType.MESH,
        )

    sent = []

    def send(k, slot, half, target, own=False):
        made = copy(k, slot, half, target, own)
        made.start()
        sent.append(made)

    def arrived(k, slot, half):
        copy(k, slot, half, me).wait_recv()

    def project(slot, own=False):
        source = tok_ref if own else held.at[rows_at(slot)]
        at = rows_at(slot)

        @pl.loop(0, 4)
        def _(i):
            cols = pl.ds(pl.multiple_of(i * 256, 256), 256)
            pre_ref[at, cols] = mm(source[...], w_pre[:, cols]).astype(B16)

        @pl.loop(0, 2)
        def _(i):
            cols = pl.ds(pl.multiple_of(i * 256, 256), 256)
            z_ref[at, cols] = mm(source[...], w_z[:, cols]).astype(B16)

        gates_ref[at, :] = mm(source[...], w_g[...]).astype(B16)

        @pl.when(slot == 7)
        def _():
            tail_copy.start()

    beside, beside_down, beside_up, beside_far = (across(i) for i in (me, down, up, far))
    send(0, me, 1, up, True)
    send(2, me, 0, down, True)
    send(4, me, 0, beside, True)
    send(5, me, 1, beside, True)
    send(1, me, 0, up, True)
    send(3, me, 1, down, True)
    for load in loads:
        load.wait()
    project(me, True)
    arrived(0, down, 1)
    send(6, down, 1, beside)
    arrived(2, up, 0)
    send(7, up, 0, beside)
    arrived(4, beside, 0)
    send(10, beside, 0, up)
    arrived(1, down, 0)
    send(8, down, 0, up)
    arrived(3, up, 1)
    send(9, up, 1, down)
    arrived(5, beside, 1)
    send(11, beside, 1, down)
    project(down)
    project(up)
    project(beside)
    arrived(10, beside_down, 0)
    send(12, beside_down, 0, up)
    arrived(11, beside_up, 1)
    send(13, beside_up, 1, down)
    arrived(8, far, 0)
    arrived(9, far, 1)
    project(far)
    arrived(6, beside_down, 1)
    project(beside_down)
    arrived(7, beside_up, 0)
    project(beside_up)
    arrived(12, beside_far, 0)
    arrived(13, beside_far, 1)
    project(beside_far)
    tail_copy.wait_recv()
    tail_ref[...] = got_tail[...]

    @pl.when(context == 0)
    def _():
        tail_ref[...] = jnp.zeros_like(tail_ref)

    tail_copy.wait_send()
    for made in sent:
        made.wait_send()


def gather_project(tokens, w_query, w_key, w_value, w_gate_z, w_gates):
    total, depth = 8 * ROWS, tokens.shape[1]
    vmem = pl.BlockSpec(memory_space=pltpu.VMEM)
    hbm = pl.BlockSpec(memory_space=pl.ANY)
    return pl.pallas_call(
        gather_kernel,
        in_specs=[vmem] + [hbm] * 5,
        out_specs=[vmem] * 4,
        out_shape=[
            jax.ShapeDtypeStruct((total, 1024), B16),
            jax.ShapeDtypeStruct((total, 512), B16),
            jax.ShapeDtypeStruct((total, 128), B16),
            jax.ShapeDtypeStruct((16, 1024), B16),
        ],
        scratch_shapes=[
            pltpu.VMEM((total, depth), B16),
            pltpu.VMEM((16, 1024), B16),
            pltpu.VMEM((depth, 1024), B16),
            pltpu.VMEM((depth, 512), B16),
            pltpu.VMEM((depth, 128), B16),
            pltpu.SemaphoreType.DMA((5,)),
            pltpu.SemaphoreType.DMA((15,)),
            pltpu.SemaphoreType.DMA((15,)),
        ],
        compiler_params=pltpu.CompilerParams(
            collective_id=0, has_side_effects=True, vmem_limit_bytes=48 * 1024 * 1024
        ),
    )(tokens, w_query, w_key, w_value, w_gate_z, w_gates)


def finish_kernel(
    op_ref, os_ref, z_ref, gain_ref, state_ref, w_ref, out_ref, part, got, send_sem, recv_sem
):
    me, up, down, far = neighbours()
    beside = across(me)
    greet({"tensor": i} for i in (up, down, beside))
    width = out_ref.shape[1]

    def share(slot, row):
        at = rows_at(row)
        normed = finish_rows(op_ref[at, :], os_ref[at, :], z_ref[at, :], gain_ref[...], state_ref)

        @pl.loop(0, width // 512)
        def _(i):
            cols = pl.ds(pl.multiple_of(i * 512, 512), 512)
            part[slot, :, cols] = mm(normed, w_ref[:, cols]).astype(B16)

    halves = (slice(0, HALF), slice(HALF, ROWS))
    sent = []

    def copy(k, slot, into, half, target):
        return pltpu.make_async_remote_copy(
            src_ref=part.at[slot, halves[half]],
            dst_ref=got.at[into, halves[half]],
            send_sem=send_sem.at[k],
            recv_sem=recv_sem.at[k],
            device_id={"tensor": target},
            device_id_type=pl.DeviceIdType.MESH,
        )

    def send(k, slot, into, half, target):
        made = copy(k, slot, into, half, target)
        made.start()
        sent.append(made)

    def arrived(k, into, half):
        copy(k, 0, into, half, me).wait_recv()

    def add(k, slot, into, half):
        arrived(k, into, half)
        rows = halves[half]
        part[slot, rows, :] = (
            part[slot, rows, :].astype(F32) + got[into, rows, :].astype(F32)
        ).astype(B16)

    share(0, across(far))
    send(0, 0, 0, 0, down)
    send(1, 0, 0, 1, up)
    share(1, across(down))
    send(2, 1, 1, 1, beside)
    share(2, across(up))
    send(3, 2, 1, 0, beside)
    share(4, far)
    share(3, beside)
    add(0, 1, 0, 0)
    send(4, 1, 2, 0, down)
    add(1, 2, 0, 1)
    send(5, 2, 2, 1, up)
    share(5, down)
    share(6, up)
    share(7, me)
    send(8, 4, 4, 0, down)
    send(9, 4, 4, 1, up)
    add(4, 3, 2, 0)
    send(6, 3, 3, 0, beside)
    add(5, 3, 2, 1)
    send(7, 3, 3, 1, beside)
    add(2, 5, 1, 1)
    send(11, 5, 5, 1, down)
    add(3, 6, 1, 0)
    send(12, 6, 6, 0, up)
    add(8, 5, 4, 0)
    send(10, 5, 5, 0, down)
    add(9, 6, 4, 1)
    send(13, 6, 6, 1, up)
    for half, ks in ((0, (6, 12, 10)), (1, (7, 11, 13))):
        for k in ks:
            arrived(k, {6: 3, 7: 3, 10: 5, 11: 5, 12: 6, 13: 6}[k], half)
        rows = halves[half]
        total = part[7, rows, :].astype(F32)
        for into in (3, 5, 6):
            total = total + got[into, rows, :].astype(F32)
        out_ref[rows, :] = total.astype(B16)
    for made in sent:
        made.wait_send()


def finish(op, os, z, gain, state, w_out):
    width = w_out.shape[1]
    vmem = pl.BlockSpec(memory_space=pltpu.VMEM)
    return pl.pallas_call(
        finish_kernel,
        in_specs=[vmem] * 6,
        out_specs=vmem,
        out_shape=jax.ShapeDtypeStruct((ROWS, width), B16),
        scratch_shapes=[
            pltpu.VMEM((8, ROWS, width), B16),
            pltpu.VMEM((7, ROWS, width), B16),
            pltpu.SemaphoreType.DMA((14,)),
            pltpu.SemaphoreType.DMA((14,)),
        ],
        compiler_params=pltpu.CompilerParams(
            collective_id=1, has_side_effects=True, vmem_limit_bytes=48 * 1024 * 1024
        ),
    )(op, os, z, gain, state, w_out)


def scan_kernel(
    x_ref, state_ref, local, pair, ring, total, before, give, back, send_sem, recv_sem
):
    me = lax.axis_index("context")
    core, z, half = me % 2, me // 2 % 8, me // 16

    def at(new_z):
        return (half * 8 + (new_z + 8) % 8) * 2 + core

    above, below = at(z + 1), at(z - 1)
    other_core = me + 1 - 2 * core
    other_half = me + 16 - 32 * half
    greet({"context": i} for i in (above, below, other_core, other_half))
    mine, theirs = pl.ds(core * 2, 2), pl.ds(2 - core * 2, 2)

    def copy(k, src, dst, target):
        return pltpu.make_async_remote_copy(
            src_ref=src,
            dst_ref=dst,
            send_sem=send_sem.at[k],
            recv_sem=recv_sem.at[k],
            device_id={"context": target},
            device_id_type=pl.DeviceIdType.MESH,
        )

    local[...] = x_ref[...].astype(B16)
    swap = copy(0, local.at[theirs], pair, other_core)
    swap.start()
    swap.wait_recv()
    first_core = core == 0
    firsts = []
    sent = [swap]
    no_add = jnp.zeros((DK, DK), F32)

    def apply(second, first):
        added = jnp.concatenate([no_add, second[:, DK:].astype(F32)], axis=1)
        return mm(second[:, :DK], first) + added

    def slot(distance, i):
        return ring.at[(z + distance + 8) % 8, i]

    def send(k, distance, i, target):
        made = copy(k, slot(distance, i), slot(distance, i), target)
        made.start()
        sent.append(made)

    def arrived(k, distance, i):
        copy(k, slot(distance, i), slot(distance, i), other_core).wait_recv()

    for i in range(2):
        own, got = local[core * 2 + i].astype(F32), pair[i].astype(F32)
        first = jnp.where(first_core, own, got).astype(B16)
        second = jnp.where(first_core, got, own).astype(B16)
        firsts.append(first)
        ring[z, i] = apply(second, first).astype(B16)
        send(1 + i, 0, i, above)
        send(3 + i, 0, i, below)
    for step in (1, 2, 3):
        for i in range(2):
            arrived(4 * step - 3 + i, -step, i)
            arrived(4 * step - 1 + i, step, i)
            if step < 3 or i == 0:
                send(4 * step + 1 + i, -step, i, above)
            if step < 3 or i == 1:
                send(4 * step + 3 + i, step, i, below)
    arrived(13, 4, 0)
    arrived(16, 4, 1)
    folded = []
    for i in range(2):
        start = lax.broadcasted_iota(jnp.int32, (DK, 2 * DK), 0) == lax.broadcasted_iota(
            jnp.int32, (DK, 2 * DK), 1
        )
        run = start.astype(F32)
        here = run
        for chip in range(8):
            here = jnp.where(z == chip, run, here)
            run = apply(ring[chip, i], run.astype(B16))
        folded.append(here)
        total[i] = run[:, DK:].astype(B16)
    onward = copy(17, total, before, other_half)

    @pl.when(half == 0)
    def _():
        before[...] = jnp.zeros_like(before)
        onward.start()
        onward.wait_send()

    @pl.when(half == 1)
    def _():
        onward.wait_recv()

    for i in range(2):
        here = folded[i]
        entering = mm(here[:, :DK].astype(B16), before[i]) + here[:, DK:]
        first = firsts[i]
        later = mm(first[:, :DK], entering.astype(B16)) + first[:, DK:].astype(F32)
        state_ref[core * 2 + i] = jnp.where(first_core, entering, later).astype(B16)
        give[i] = jnp.where(first_core, later, entering).astype(B16)
    swap_back = copy(18, give, back, other_core)
    swap_back.start()
    swap_back.wait()
    for i in range(2):
        state_ref[2 - core * 2 + i] = back[i]
    for made in sent:
        made.wait_send()


def entering_state(x):
    vmem = pl.BlockSpec(memory_space=pltpu.VMEM)
    return pl.pallas_call(
        scan_kernel,
        in_specs=[vmem],
        out_specs=vmem,
        out_shape=jax.ShapeDtypeStruct((HEADS, DK, DV), B16),
        scratch_shapes=[
            pltpu.VMEM((HEADS, DK, 2 * DK), B16),
            pltpu.VMEM((2, DK, 2 * DK), B16),
            pltpu.VMEM((8, 2, DK, 2 * DK), B16),
            pltpu.VMEM((2, DK, DV), B16),
            pltpu.VMEM((2, DK, DV), B16),
            pltpu.VMEM((2, DK, DV), B16),
            pltpu.VMEM((2, DK, DV), B16),
            pltpu.SemaphoreType.DMA((19,)),
            pltpu.SemaphoreType.DMA((19,)),
        ],
        compiler_params=pltpu.CompilerParams(
            collective_id=2, has_side_effects=True, vmem_limit_bytes=48 * 1024 * 1024
        ),
    )(x)


def gate_weights(w_gates):
    order = w_gates.transpose(0, 2, 1).reshape(w_gates.shape[0], 2 * HEADS)
    return jnp.pad(order, ((0, 0), (0, 128 - 2 * HEADS)))


def small_inputs(conv_query, conv_key, conv_value, a_log, dt_bias, norm_gain):
    taps = jnp.concatenate([conv_query, conv_key, conv_value], axis=1).astype(F32)
    taps = jnp.pad(taps, ((0, 8 - KW), (0, 0)))
    par = jnp.pad(jnp.stack([a_log, dt_bias]), ((0, 6), (0, 128 - HEADS)))
    return taps, par, norm_gain.astype(F32)[None, :]


def per_device(
    tokens,
    w_query,
    w_key,
    w_value,
    w_gate_z,
    w_gates,
    conv_query,
    conv_key,
    conv_value,
    a_log,
    dt_bias,
    norm_gain,
    w_out,
):
    taps, par, gain = small_inputs(conv_query, conv_key, conv_value, a_log, dt_bias, norm_gain)
    pre, z, gates, tail = gather_project(
        tokens, w_query, w_key, w_value, w_gate_z, gate_weights(w_gates)
    )
    op, os, x = local_pass(pre, tail, gates, taps, par)
    state = entering_state(x)
    return finish(op, os, z, gain, state, w_out)


def solution(mesh):
    placed = (
        P(("context", "tensor"), None),
        P(None, "tensor"),
        P(None, "tensor"),
        P(None, "tensor"),
        P(None, "tensor"),
        P(None, "tensor", None),
        P(None, "tensor"),
        P(None, "tensor"),
        P(None, "tensor"),
        P("tensor"),
        P("tensor"),
        P(),
        P("tensor", None),
    )
    return jax.shard_map(
        per_device,
        mesh=mesh,
        in_specs=placed,
        out_specs=P(("context", "tensor"), None),
        check_vma=False,
    )
```

```python
import functools

import jax
import jax.numpy as jnp
from jax import lax
from jax.experimental import pallas as pl
from jax.experimental.pallas import tpu as pltpu
from jax.sharding import PartitionSpec as P

HK = 16
HV = 32
DK = 128
DV = 128
KW = 4
EPSILON = 1e-06
LEN = 128
PER_STEP = 5
SOLVE = 64
HEADS = 4
KEYS = 2
ROWS = 160
HALF = 80
F32 = jnp.float32
B16 = jnp.bfloat16


def mm(a, b):
    return jnp.dot(a, b, preferred_element_type=F32)


def mm_nt(a, b):
    return lax.dot_general(a, b, (((1,), (1,)), ((), ())), preferred_element_type=F32)


def mm_tn(a, b):
    return lax.dot_general(a, b, (((0,), (0,)), ((), ())), preferred_element_type=F32)


def silu(x):
    return x / (1.0 + jnp.exp(-x))


def unit(x):
    return x * lax.rsqrt(jnp.sum(x * x, axis=-1, keepdims=True) + EPSILON)


def chunk_terms(convs, gates, gate_par):
    ii = lax.broadcasted_iota(jnp.int32, (LEN, LEN), 0)
    jj = lax.broadcasted_iota(jnp.int32, (LEN, LEN), 1)
    lower = (ii >= jj).astype(F32)
    strict = (ii > jj).astype(F32)
    differ = ii ^ jj
    levels = [((differ >> s) == 1).astype(B16) for s in range(SOLVE.bit_length() - 1)]
    eye = (ii == jj).astype(B16)

    units = []
    for conv in convs:
        for g in range(KEYS):
            qf = unit(conv[:, g * DK : (g + 1) * DK]) * (DK**-0.5)
            kf = unit(conv[:, 256 + g * DK : 256 + (g + 1) * DK])
            units.append((qf, kf, qf.astype(B16), kf.astype(B16)))
    kks = [mm_nt(kb, kb) * strict for _, _, _, kb in units]
    qks = [mm_nt(qb, kb) * lower for _, _, qb, kb in units]

    logits = [gate.astype(F32) for gate in gates]
    shifted = [x + gate_par[1:2, :] for x in logits]
    softplus = [jnp.maximum(x, 0.0) + jnp.log1p(jnp.exp(-jnp.abs(x))) for x in shifted]
    rate = -jnp.exp(gate_par[0:1, :])
    cums = [
        jnp.dot(lower, rate * x, preferred_element_type=F32, precision=lax.Precision.HIGHEST)
        for x in softplus
    ]

    terms = []
    for c, (conv, cum) in enumerate(zip(convs, cums)):
        beta = 1.0 / (1.0 + jnp.exp(-logits[c]))
        cum_t = cum.T
        growth = jnp.exp(cum)
        fade = jnp.exp(cum[LEN - 1 : LEN, :] - cum)
        for h in range(HEADS):
            qf, kf, _, _ = units[c * KEYS + h // 2]
            kk, qk = kks[c * KEYS + h // 2], qks[c * KEYS + h // 2]
            spread = jnp.exp(jnp.minimum(cum[:, h : h + 1] - cum_t[h : h + 1, :], 0.0))
            b = beta[:, 4 + h : 5 + h]
            a = (kk * spread * b).astype(B16)
            r = (qk * spread).astype(B16)
            vb = (conv[:, 512 + h * DV : 512 + (h + 1) * DV] * b).astype(B16)
            grow = growth[:, h : h + 1]
            src = jnp.concatenate([(kf * (b * grow)).astype(B16), vb], axis=1)
            fk = (kf * fade[:, h : h + 1]).astype(B16)
            terms.append((a, r, src, fk, qf * grow, growth[LEN - 1 : LEN, h : h + 1]))
    inv = [eye - t[0] * levels[0] for t in terms]
    for level in levels[1:]:
        part = [mm(t[0] * level, x).astype(B16) for t, x in zip(terms, inv)]
        inv = [x - mm(x, p).astype(B16) for x, p in zip(inv, part)]
    found = [[] for _ in terms]
    for i in range(LEN // SOLVE):
        rows = slice(i * SOLVE, (i + 1) * SOLVE)
        rhs = [t[2][rows] for t in terms]
        if i:
            known = [jnp.concatenate(f, axis=0) if i > 1 else f[0] for f in found]
            rhs = [
                (x.astype(F32) - mm(t[0][rows, : i * SOLVE], k)).astype(B16)
                for t, x, k in zip(terms, rhs, known)
            ]
        for f, x, y in zip(found, inv, rhs):
            f.append(mm(x[rows, rows], y).astype(B16))
    yws = [jnp.concatenate(f, axis=0) for f in found]
    fyws = [mm_tn(t[3], yw) for t, yw in zip(terms, yws)]
    ryws = [mm(t[1], yw) for t, yw in zip(terms, yws)]
    return [
        ((t[4] - ryw[:, :DK]).astype(B16), ryw[:, DK:], fyw[:, :DK].astype(B16), fyw[:, DK:], t[5])
        for t, ryw, fyw in zip(terms, ryws, fyws)
    ]


def local_kernel(pre_ref, tail_ref, gates_ref, taps_ref, par_ref, op_ref, os_ref, x_ref, ext):
    step = pl.program_id(0)
    rows = LEN * PER_STEP

    @pl.when(step == 0)
    def _():
        ext[0:8, :] = tail_ref[...].astype(F32)[8:16, :]
        eye = lax.broadcasted_iota(jnp.int32, (DK, 2 * DK), 0) == lax.broadcasted_iota(
            jnp.int32, (DK, 2 * DK), 1
        )
        for h in range(HEADS):
            x_ref[h] = eye.astype(F32)

    @pl.when(step > 0)
    def _():
        ext[0:8, :] = ext[rows : rows + 8, :]

    ext[8 : rows + 8, :] = pre_ref[...].astype(F32)
    taps = taps_ref[...]
    par = par_ref[...]
    convs = []
    for c in range(PER_STEP):
        base = c * LEN + 8
        conv = taps[0:1, :] * ext[base - 3 : base - 3 + LEN, :]
        for j in range(1, KW):
            conv = conv + taps[j : j + 1, :] * ext[base - 3 + j : base - 3 + j + LEN, :]
        convs.append(silu(conv))
    gates = [gates_ref[c * LEN : (c + 1) * LEN, :] for c in range(PER_STEP)]
    done = chunk_terms(convs, gates, par)
    xs = [x_ref[h] for h in range(HEADS)]
    for c in range(PER_STEP):
        at = slice(c * LEN, (c + 1) * LEN)
        now = done[c * HEADS : (c + 1) * HEADS]
        xbs = [x.astype(B16) for x in xs]
        moved = [mm(d[2], xb) for d, xb in zip(now, xbs)]
        seen = [mm(d[0], xb) for d, xb in zip(now, xbs)]
        for h in range(HEADS):
            cols = slice(h * DV, (h + 1) * DV)
            op_ref[at, cols] = seen[h][:, :DK].astype(B16)
            os_ref[at, cols] = seen[h][:, DK:] + now[h][1]
            x = xs[h] * now[h][4] - moved[h]
            xs[h] = jnp.concatenate([x[:, :DK], x[:, DK:] + now[h][3]], axis=1)
    for h in range(HEADS):
        x_ref[h] = xs[h]


def local_pass(pre, tail, gates, taps, par):
    rows = LEN * PER_STEP
    total = pre.shape[0]
    return pl.pallas_call(
        local_kernel,
        grid=(total // rows,),
        in_specs=[
            pl.BlockSpec((rows, 1024), lambda i: (i, 0)),
            pl.BlockSpec((16, 1024), lambda i: (0, 0)),
            pl.BlockSpec((rows, 128), lambda i: (i, 0)),
            pl.BlockSpec((8, 1024), lambda i: (0, 0)),
            pl.BlockSpec((8, 128), lambda i: (0, 0)),
        ],
        out_specs=[
            pl.BlockSpec((rows, 512), lambda i: (i, 0)),
            pl.BlockSpec((rows, 512), lambda i: (i, 0)),
            pl.BlockSpec((HEADS, DK, 2 * DK), lambda i: (0, 0, 0)),
        ],
        out_shape=[
            jax.ShapeDtypeStruct((total, 512), B16),
            jax.ShapeDtypeStruct((total, 512), F32),
            jax.ShapeDtypeStruct((HEADS, DK, 2 * DK), F32),
        ],
        scratch_shapes=[pltpu.VMEM((rows + 8, 1024), F32)],
        compiler_params=pltpu.CompilerParams(
            dimension_semantics=("arbitrary",), vmem_limit_bytes=48 * 1024 * 1024
        ),
    )(pre, tail, gates, taps, par)


def finish_rows(seen, own, z, gain, state):
    parts = []
    for h in range(HEADS):
        cols = slice(h * DV, (h + 1) * DV)
        core = mm(seen[:, cols], state[h]) + own[:, cols]
        scale = lax.rsqrt(jnp.mean(core * core, axis=-1, keepdims=True) + EPSILON)
        parts.append((core * scale * gain * silu(z[:, cols].astype(F32))).astype(B16))
    return jnp.concatenate(parts, axis=1)


def neighbours():
    me = lax.axis_index("tensor")
    y, x = me // 2, me % 2
    up, down, far = ((y + d) % 4 * 2 + x for d in (1, 3, 2))
    return me, up, down, far


def across(index):
    return index // 2 * 2 + 1 - index % 2


def greet(partners):
    barrier = pltpu.get_barrier_semaphore()
    partners = tuple(partners)
    for partner in partners:
        pl.semaphore_signal(
            barrier, inc=1, device_id=partner, device_id_type=pl.DeviceIdType.MESH
        )
    return lambda: pl.semaphore_wait(barrier, len(partners))


def rows_at(index, half=None):
    if half is None:
        return pl.ds(pl.multiple_of(index * ROWS, 16), ROWS)
    return pl.ds(pl.multiple_of(index * ROWS + half * HALF, 16), HALF)


def gather_kernel(
    tok_ref, wq_ref, wk_ref, wv_ref, wz_ref, wg_ref, pre_ref, z_ref, gates_ref, tail_ref,
    held, got_tail, w_pre, w_z, w_g, w_sem, send_sem, recv_sem,
):
    me, up, down, far = neighbours()
    loads = [
        pltpu.make_async_copy(src, dst, w_sem.at[i])
        for i, (src, dst) in enumerate(
            (
                (wq_ref, w_pre.at[:, 0:256]),
                (wk_ref, w_pre.at[:, 256:512]),
                (wv_ref, w_pre.at[:, 512:1024]),
                (wz_ref, w_z),
                (wg_ref, w_g),
            )
        )
    ]
    context = lax.axis_index("context")
    after = (context + 1) % 32
    all_here = greet(
        [{"tensor": i} for i in (up, down, across(me))]
        + [{"context": i} for i in (after, (context + 31) % 32)]
    )
    for load in loads:
        load.start()
    all_here()
    tail_copy = pltpu.make_async_remote_copy(
        src_ref=pre_ref.at[8 * ROWS - 16 : 8 * ROWS],
        dst_ref=got_tail,
        send_sem=send_sem.at[14],
        recv_sem=recv_sem.at[14],
        device_id={"context": after},
        device_id_type=pl.DeviceIdType.MESH,
    )

    def copy(k, slot, half, target, own=False):
        return pltpu.make_async_remote_copy(
            src_ref=tok_ref.at[half * HALF : half * HALF + HALF] if own else held.at[rows_at(slot, half)],
            dst_ref=held.at[rows_at(slot, half)],
            send_sem=send_sem.at[k],
            recv_sem=recv_sem.at[k],
            device_id={"tensor": target},
            device_id_type=pl.DeviceIdType.MESH,
        )

    sent = []

    def send(k, slot, half, target, own=False):
        made = copy(k, slot, half, target, own)
        made.start()
        sent.append(made)

    def arrived(k, slot, half):
        copy(k, slot, half, me).wait_recv()

    def project(slot, own=False):
        source = tok_ref if own else held.at[rows_at(slot)]
        at = rows_at(slot)

        @pl.loop(0, 4)
        def _(i):
            cols = pl.ds(pl.multiple_of(i * 256, 256), 256)
            pre_ref[at, cols] = mm(source[...], w_pre[:, cols]).astype(B16)

        @pl.loop(0, 2)
        def _(i):
            cols = pl.ds(pl.multiple_of(i * 256, 256), 256)
            z_ref[at, cols] = mm(source[...], w_z[:, cols]).astype(B16)

        gates_ref[at, :] = mm(source[...], w_g[...]).astype(B16)

        @pl.when(slot == 7)
        def _():
            tail_copy.start()

    beside, beside_down, beside_up, beside_far = (across(i) for i in (me, down, up, far))
    send(0, me, 1, up, True)
    send(2, me, 0, down, True)
    send(4, me, 0, beside, True)
    send(5, me, 1, beside, True)
    send(1, me, 0, up, True)
    send(3, me, 1, down, True)
    for load in loads:
        load.wait()
    project(me, True)
    arrived(0, down, 1)
    send(6, down, 1, beside)
    arrived(2, up, 0)
    send(7, up, 0, beside)
    arrived(4, beside, 0)
    send(10, beside, 0, up)
    arrived(1, down, 0)
    send(8, down, 0, up)
    arrived(3, up, 1)
    send(9, up, 1, down)
    arrived(5, beside, 1)
    send(11, beside, 1, down)
    project(down)
    project(up)
    project(beside)
    arrived(10, beside_down, 0)
    send(12, beside_down, 0, up)
    arrived(11, beside_up, 1)
    send(13, beside_up, 1, down)
    arrived(8, far, 0)
    arrived(9, far, 1)
    project(far)
    arrived(6, beside_down, 1)
    project(beside_down)
    arrived(7, beside_up, 0)
    project(beside_up)
    arrived(12, beside_far, 0)
    arrived(13, beside_far, 1)
    project(beside_far)
    tail_copy.wait_recv()
    tail_ref[...] = got_tail[...]

    @pl.when(context == 0)
    def _():
        tail_ref[...] = jnp.zeros_like(tail_ref)

    tail_copy.wait_send()
    for made in sent:
        made.wait_send()


def gather_project(tokens, w_query, w_key, w_value, w_gate_z, w_gates):
    total, depth = 8 * ROWS, tokens.shape[1]
    vmem = pl.BlockSpec(memory_space=pltpu.VMEM)
    hbm = pl.BlockSpec(memory_space=pl.ANY)
    return pl.pallas_call(
        gather_kernel,
        in_specs=[vmem] + [hbm] * 5,
        out_specs=[vmem] * 4,
        out_shape=[
            jax.ShapeDtypeStruct((total, 1024), B16),
            jax.ShapeDtypeStruct((total, 512), B16),
            jax.ShapeDtypeStruct((total, 128), B16),
            jax.ShapeDtypeStruct((16, 1024), B16),
        ],
        scratch_shapes=[
            pltpu.VMEM((total, depth), B16),
            pltpu.VMEM((16, 1024), B16),
            pltpu.VMEM((depth, 1024), B16),
            pltpu.VMEM((depth, 512), B16),
            pltpu.VMEM((depth, 128), B16),
            pltpu.SemaphoreType.DMA((5,)),
            pltpu.SemaphoreType.DMA((15,)),
            pltpu.SemaphoreType.DMA((15,)),
        ],
        compiler_params=pltpu.CompilerParams(
            collective_id=0, has_side_effects=True, vmem_limit_bytes=48 * 1024 * 1024
        ),
    )(tokens, w_query, w_key, w_value, w_gate_z, w_gates)


def finish_kernel(
    op_ref, os_ref, z_ref, gain_ref, state_ref, w_ref, out_ref, part, got, send_sem, recv_sem
):
    me, up, down, far = neighbours()
    beside = across(me)
    all_here = greet({"tensor": i} for i in (up, down, beside))
    width = out_ref.shape[1]

    def share(slot, row):
        at = rows_at(row)
        normed = finish_rows(op_ref[at, :], os_ref[at, :], z_ref[at, :], gain_ref[...], state_ref)

        @pl.loop(0, width // 512)
        def _(i):
            cols = pl.ds(pl.multiple_of(i * 512, 512), 512)
            part[slot, :, cols] = mm(normed, w_ref[:, cols]).astype(B16)

    halves = (slice(0, HALF), slice(HALF, ROWS))
    sent = []

    def copy(k, slot, into, half, target):
        return pltpu.make_async_remote_copy(
            src_ref=part.at[slot, halves[half]],
            dst_ref=got.at[into, halves[half]],
            send_sem=send_sem.at[k],
            recv_sem=recv_sem.at[k],
            device_id={"tensor": target},
            device_id_type=pl.DeviceIdType.MESH,
        )

    def send(k, slot, into, half, target):
        made = copy(k, slot, into, half, target)
        made.start()
        sent.append(made)

    def arrived(k, into, half):
        copy(k, 0, into, half, me).wait_recv()

    def add(k, slot, into, half):
        arrived(k, into, half)
        rows = halves[half]
        part[slot, rows, :] = (
            part[slot, rows, :].astype(F32) + got[into, rows, :].astype(F32)
        ).astype(B16)

    share(0, across(far))
    all_here()
    send(0, 0, 0, 0, down)
    send(1, 0, 0, 1, up)
    share(1, across(down))
    send(2, 1, 1, 1, beside)
    share(2, across(up))
    send(3, 2, 1, 0, beside)
    share(4, far)
    share(3, beside)
    add(0, 1, 0, 0)
    send(4, 1, 2, 0, down)
    add(1, 2, 0, 1)
    send(5, 2, 2, 1, up)
    share(5, down)
    share(6, up)
    share(7, me)
    send(8, 4, 4, 0, down)
    send(9, 4, 4, 1, up)
    add(4, 3, 2, 0)
    send(6, 3, 3, 0, beside)
    add(5, 3, 2, 1)
    send(7, 3, 3, 1, beside)
    add(2, 5, 1, 1)
    send(11, 5, 5, 1, down)
    add(3, 6, 1, 0)
    send(12, 6, 6, 0, up)
    add(8, 5, 4, 0)
    send(10, 5, 5, 0, down)
    add(9, 6, 4, 1)
    send(13, 6, 6, 1, up)
    for half, ks in ((0, (6, 12, 10)), (1, (7, 11, 13))):
        for k in ks:
            arrived(k, {6: 3, 7: 3, 10: 5, 11: 5, 12: 6, 13: 6}[k], half)
        rows = halves[half]
        total = part[7, rows, :].astype(F32)
        for into in (3, 5, 6):
            total = total + got[into, rows, :].astype(F32)
        out_ref[rows, :] = total.astype(B16)
    for made in sent:
        made.wait_send()


def finish(op, os, z, gain, state, w_out):
    width = w_out.shape[1]
    vmem = pl.BlockSpec(memory_space=pltpu.VMEM)
    return pl.pallas_call(
        finish_kernel,
        in_specs=[vmem] * 6,
        out_specs=vmem,
        out_shape=jax.ShapeDtypeStruct((ROWS, width), B16),
        scratch_shapes=[
            pltpu.VMEM((8, ROWS, width), B16),
            pltpu.VMEM((7, ROWS, width), B16),
            pltpu.SemaphoreType.DMA((14,)),
            pltpu.SemaphoreType.DMA((14,)),
        ],
        compiler_params=pltpu.CompilerParams(
            collective_id=1, has_side_effects=True, vmem_limit_bytes=28 * 1024 * 1024
        ),
    )(op, os, z, gain, state, w_out)


def scan_kernel(
    x_ref, state_ref, local, pair, ring, total, before, give, back, send_sem, recv_sem
):
    me = lax.axis_index("context")
    core, z, half = me % 2, me // 2 % 8, me // 16

    def at(new_z):
        return (half * 8 + (new_z + 8) % 8) * 2 + core

    above, below = at(z + 1), at(z - 1)
    other_core = me + 1 - 2 * core
    other_half = me + 16 - 32 * half
    all_here = greet({"context": i} for i in (above, below, other_core, other_half))
    mine, theirs = pl.ds(core * 2, 2), pl.ds(2 - core * 2, 2)

    def copy(k, src, dst, target):
        return pltpu.make_async_remote_copy(
            src_ref=src,
            dst_ref=dst,
            send_sem=send_sem.at[k],
            recv_sem=recv_sem.at[k],
            device_id={"context": target},
            device_id_type=pl.DeviceIdType.MESH,
        )

    local[...] = x_ref[...].astype(B16)
    all_here()
    swap = copy(0, local.at[theirs], pair, other_core)
    swap.start()
    swap.wait_recv()
    first_core = core == 0
    firsts = []
    sent = [swap]
    no_add = jnp.zeros((DK, DK), F32)

    def apply(second, first):
        added = jnp.concatenate([no_add, second[:, DK:].astype(F32)], axis=1)
        return mm(second[:, :DK], first) + added

    def slot(distance, i):
        return ring.at[(z + distance + 8) % 8, i]

    def send(k, distance, i, target):
        made = copy(k, slot(distance, i), slot(distance, i), target)
        made.start()
        sent.append(made)

    def arrived(k, distance, i):
        copy(k, slot(distance, i), slot(distance, i), other_core).wait_recv()

    for i in range(2):
        own, got = local[core * 2 + i].astype(F32), pair[i].astype(F32)
        first = jnp.where(first_core, own, got).astype(B16)
        second = jnp.where(first_core, got, own).astype(B16)
        firsts.append(first)
        ring[z, i] = apply(second, first).astype(B16)
        send(1 + i, 0, i, above)
        send(3 + i, 0, i, below)
    for step in (1, 2, 3):
        for i in range(2):
            arrived(4 * step - 3 + i, -step, i)
            arrived(4 * step - 1 + i, step, i)
            if step < 3 or i == 0:
                send(4 * step + 1 + i, -step, i, above)
            if step < 3 or i == 1:
                send(4 * step + 3 + i, step, i, below)
    arrived(13, 4, 0)
    arrived(16, 4, 1)
    folded = []
    for i in range(2):
        start = lax.broadcasted_iota(jnp.int32, (DK, 2 * DK), 0) == lax.broadcasted_iota(
            jnp.int32, (DK, 2 * DK), 1
        )
        run = start.astype(F32)
        here = run
        for chip in range(8):
            here = jnp.where(z == chip, run, here)
            run = apply(ring[chip, i], run.astype(B16))
        folded.append(here)
        total[i] = run[:, DK:].astype(B16)
    onward = copy(17, total, before, other_half)

    @pl.when(half == 0)
    def _():
        before[...] = jnp.zeros_like(before)
        onward.start()
        onward.wait_send()

    @pl.when(half == 1)
    def _():
        onward.wait_recv()

    for i in range(2):
        here = folded[i]
        entering = mm(here[:, :DK].astype(B16), before[i]) + here[:, DK:]
        first = firsts[i]
        later = mm(first[:, :DK], entering.astype(B16)) + first[:, DK:].astype(F32)
        state_ref[core * 2 + i] = jnp.where(first_core, entering, later).astype(B16)
        give[i] = jnp.where(first_core, later, entering).astype(B16)
    swap_back = copy(18, give, back, other_core)
    swap_back.start()
    swap_back.wait()
    for i in range(2):
        state_ref[2 - core * 2 + i] = back[i]
    for made in sent:
        made.wait_send()


def entering_state(x):
    vmem = pl.BlockSpec(memory_space=pltpu.VMEM)
    return pl.pallas_call(
        scan_kernel,
        in_specs=[vmem],
        out_specs=vmem,
        out_shape=jax.ShapeDtypeStruct((HEADS, DK, DV), B16),
        scratch_shapes=[
            pltpu.VMEM((HEADS, DK, 2 * DK), B16),
            pltpu.VMEM((2, DK, 2 * DK), B16),
            pltpu.VMEM((8, 2, DK, 2 * DK), B16),
            pltpu.VMEM((2, DK, DV), B16),
            pltpu.VMEM((2, DK, DV), B16),
            pltpu.VMEM((2, DK, DV), B16),
            pltpu.VMEM((2, DK, DV), B16),
            pltpu.SemaphoreType.DMA((19,)),
            pltpu.SemaphoreType.DMA((19,)),
        ],
        compiler_params=pltpu.CompilerParams(
            collective_id=2, has_side_effects=True, vmem_limit_bytes=8 * 1024 * 1024
        ),
    )(x)


def gate_weights(w_gates):
    order = w_gates.transpose(0, 2, 1).reshape(w_gates.shape[0], 2 * HEADS)
    return jnp.pad(order, ((0, 0), (0, 128 - 2 * HEADS)))


def small_inputs(conv_query, conv_key, conv_value, a_log, dt_bias, norm_gain):
    taps = jnp.concatenate([conv_query, conv_key, conv_value], axis=1).astype(F32)
    taps = jnp.pad(taps, ((0, 8 - KW), (0, 0)))
    par = jnp.pad(jnp.stack([a_log, dt_bias]), ((0, 6), (0, 128 - HEADS)))
    return taps, par, norm_gain.astype(F32)[None, :]


def per_device(
    tokens,
    w_query,
    w_key,
    w_value,
    w_gate_z,
    w_gates,
    conv_query,
    conv_key,
    conv_value,
    a_log,
    dt_bias,
    norm_gain,
    w_out,
):
    taps, par, gain = small_inputs(conv_query, conv_key, conv_value, a_log, dt_bias, norm_gain)
    pre, z, gates, tail = gather_project(
        tokens, w_query, w_key, w_value, w_gate_z, gate_weights(w_gates)
    )
    op, os, x = local_pass(pre, tail, gates, taps, par)
    state = entering_state(x)
    return finish(op, os, z, gain, state, w_out)


def solution(mesh):
    placed = (
        P(("context", "tensor"), None),
        P(None, "tensor"),
        P(None, "tensor"),
        P(None, "tensor"),
        P(None, "tensor"),
        P(None, "tensor", None),
        P(None, "tensor"),
        P(None, "tensor"),
        P(None, "tensor"),
        P("tensor"),
        P("tensor"),
        P(),
        P("tensor", None),
    )
    return jax.shard_map(
        per_device,
        mesh=mesh,
        in_specs=placed,
        out_specs=P(("context", "tensor"), None),
        check_vma=False,
    )
```

```python
import functools

import jax
import jax.numpy as jnp
from jax import lax
from jax.experimental import pallas as pl
from jax.experimental.pallas import tpu as pltpu
from jax.sharding import PartitionSpec as P

HK = 16
HV = 32
DK = 128
DV = 128
KW = 4
EPSILON = 1e-06
LEN = 128
PER_STEP = 5
SOLVE = 64
HEADS = 4
KEYS = 2
ROWS = 160
HALF = 80
F32 = jnp.float32
B16 = jnp.bfloat16


def mm(a, b):
    return jnp.dot(a, b, preferred_element_type=F32)


def mm_nt(a, b):
    return lax.dot_general(a, b, (((1,), (1,)), ((), ())), preferred_element_type=F32)


def mm_tn(a, b):
    return lax.dot_general(a, b, (((0,), (0,)), ((), ())), preferred_element_type=F32)


def silu(x):
    return x / (1.0 + jnp.exp(-x))


def unit(x):
    return x * lax.rsqrt(jnp.sum(x * x, axis=-1, keepdims=True) + EPSILON)


def chunk_terms(convs, gates, gate_par):
    ii = lax.broadcasted_iota(jnp.int32, (LEN, LEN), 0)
    jj = lax.broadcasted_iota(jnp.int32, (LEN, LEN), 1)
    lower = (ii >= jj).astype(F32)
    strict = (ii > jj).astype(F32)
    differ = ii ^ jj
    levels = [((differ >> s) == 1).astype(B16) for s in range(SOLVE.bit_length() - 1)]
    eye = (ii == jj).astype(B16)

    units = []
    for conv in convs:
        for g in range(KEYS):
            qf = unit(conv[:, g * DK : (g + 1) * DK]) * (DK**-0.5)
            kf = unit(conv[:, 256 + g * DK : 256 + (g + 1) * DK])
            units.append((qf, kf, qf.astype(B16), kf.astype(B16)))
    kks = [mm_nt(kb, kb) * strict for _, _, _, kb in units]
    qks = [mm_nt(qb, kb) * lower for _, _, qb, kb in units]

    logits = [gate.astype(F32) for gate in gates]
    shifted = [x + gate_par[1:2, :] for x in logits]
    softplus = [jnp.maximum(x, 0.0) + jnp.log1p(jnp.exp(-jnp.abs(x))) for x in shifted]
    rate = -jnp.exp(gate_par[0:1, :])
    cums = [
        jnp.dot(lower, rate * x, preferred_element_type=F32, precision=lax.Precision.HIGHEST)
        for x in softplus
    ]

    terms = []
    for c, (conv, cum) in enumerate(zip(convs, cums)):
        beta = 1.0 / (1.0 + jnp.exp(-logits[c]))
        cum_t = cum.T
        growth = jnp.exp(cum)
        fade = jnp.exp(cum[LEN - 1 : LEN, :] - cum)
        for h in range(HEADS):
            qf, kf, _, _ = units[c * KEYS + h // 2]
            kk, qk = kks[c * KEYS + h // 2], qks[c * KEYS + h // 2]
            spread = jnp.exp(jnp.minimum(cum[:, h : h + 1] - cum_t[h : h + 1, :], 0.0))
            b = beta[:, 4 + h : 5 + h]
            a = (kk * spread * b).astype(B16)
            r = (qk * spread).astype(B16)
            vb = (conv[:, 512 + h * DV : 512 + (h + 1) * DV] * b).astype(B16)
            grow = growth[:, h : h + 1]
            src = jnp.concatenate([(kf * (b * grow)).astype(B16), vb], axis=1)
            fk = (kf * fade[:, h : h + 1]).astype(B16)
            terms.append((a, r, src, fk, qf * grow, growth[LEN - 1 : LEN, h : h + 1]))
    inv = [eye - t[0] * levels[0] for t in terms]
    for level in levels[1:]:
        part = [mm(t[0] * level, x).astype(B16) for t, x in zip(terms, inv)]
        inv = [x - mm(x, p).astype(B16) for x, p in zip(inv, part)]
    found = [[] for _ in terms]
    for i in range(LEN // SOLVE):
        rows = slice(i * SOLVE, (i + 1) * SOLVE)
        rhs = [t[2][rows] for t in terms]
        if i:
            known = [jnp.concatenate(f, axis=0) if i > 1 else f[0] for f in found]
            rhs = [
                (x.astype(F32) - mm(t[0][rows, : i * SOLVE], k)).astype(B16)
                for t, x, k in zip(terms, rhs, known)
            ]
        for f, x, y in zip(found, inv, rhs):
            f.append(mm(x[rows, rows], y).astype(B16))
    yws = [jnp.concatenate(f, axis=0) for f in found]
    fyws = [mm_tn(t[3], yw) for t, yw in zip(terms, yws)]
    ryws = [mm(t[1], yw) for t, yw in zip(terms, yws)]
    return [
        ((t[4] - ryw[:, :DK]).astype(B16), ryw[:, DK:], fyw[:, :DK].astype(B16), fyw[:, DK:], t[5])
        for t, ryw, fyw in zip(terms, ryws, fyws)
    ]


def local_kernel(pre_ref, tail_ref, gates_ref, taps_ref, par_ref, op_ref, os_ref, x_ref, ext):
    step = pl.program_id(0)
    rows = LEN * PER_STEP

    @pl.when(step == 0)
    def _():
        ext[0:8, :] = tail_ref[...].astype(F32)[8:16, :]
        eye = lax.broadcasted_iota(jnp.int32, (DK, 2 * DK), 0) == lax.broadcasted_iota(
            jnp.int32, (DK, 2 * DK), 1
        )
        for h in range(HEADS):
            x_ref[h] = eye.astype(F32)

    @pl.when(step > 0)
    def _():
        ext[0:8, :] = ext[rows : rows + 8, :]

    ext[8 : rows + 8, :] = pre_ref[...].astype(F32)
    taps = taps_ref[...]
    par = par_ref[...]
    convs = []
    for c in range(PER_STEP):
        base = c * LEN + 8
        conv = taps[0:1, :] * ext[base - 3 : base - 3 + LEN, :]
        for j in range(1, KW):
            conv = conv + taps[j : j + 1, :] * ext[base - 3 + j : base - 3 + j + LEN, :]
        convs.append(silu(conv))
    gates = [gates_ref[c * LEN : (c + 1) * LEN, :] for c in range(PER_STEP)]
    done = chunk_terms(convs, gates, par)
    xs = [x_ref[h] for h in range(HEADS)]
    for c in range(PER_STEP):
        at = slice(c * LEN, (c + 1) * LEN)
        now = done[c * HEADS : (c + 1) * HEADS]
        xbs = [x.astype(B16) for x in xs]
        moved = [mm(d[2], xb) for d, xb in zip(now, xbs)]
        seen = [mm(d[0], xb) for d, xb in zip(now, xbs)]
        for h in range(HEADS):
            cols = slice(h * DV, (h + 1) * DV)
            op_ref[at, cols] = seen[h][:, :DK].astype(B16)
            os_ref[at, cols] = seen[h][:, DK:] + now[h][1]
            x = xs[h] * now[h][4] - moved[h]
            xs[h] = jnp.concatenate([x[:, :DK], x[:, DK:] + now[h][3]], axis=1)
    for h in range(HEADS):
        x_ref[h] = xs[h]


def local_pass(pre, tail, gates, taps, par):
    rows = LEN * PER_STEP
    total = pre.shape[0]
    return pl.pallas_call(
        local_kernel,
        grid=(total // rows,),
        in_specs=[
            pl.BlockSpec((rows, 1024), lambda i: (i, 0)),
            pl.BlockSpec((16, 1024), lambda i: (0, 0)),
            pl.BlockSpec((rows, 128), lambda i: (i, 0)),
            pl.BlockSpec((8, 1024), lambda i: (0, 0)),
            pl.BlockSpec((8, 128), lambda i: (0, 0)),
        ],
        out_specs=[
            pl.BlockSpec((rows, 512), lambda i: (i, 0)),
            pl.BlockSpec((rows, 512), lambda i: (i, 0)),
            pl.BlockSpec((HEADS, DK, 2 * DK), lambda i: (0, 0, 0)),
        ],
        out_shape=[
            jax.ShapeDtypeStruct((total, 512), B16),
            jax.ShapeDtypeStruct((total, 512), F32),
            jax.ShapeDtypeStruct((HEADS, DK, 2 * DK), F32),
        ],
        scratch_shapes=[pltpu.VMEM((rows + 8, 1024), F32)],
        compiler_params=pltpu.CompilerParams(
            dimension_semantics=("arbitrary",), vmem_limit_bytes=48 * 1024 * 1024
        ),
    )(pre, tail, gates, taps, par)


def finish_rows(seen, own, z, gain, state):
    parts = []
    heads = [slice(h * DV, (h + 1) * DV) for h in range(HEADS)]
    cores = [mm(seen[:, cols], state[h]) + own[:, cols] for h, cols in enumerate(heads)]
    for core, cols in zip(cores, heads):
        scale = lax.rsqrt(jnp.mean(core * core, axis=-1, keepdims=True) + EPSILON)
        parts.append((core * scale * gain * silu(z[:, cols].astype(F32))).astype(B16))
    return jnp.concatenate(parts, axis=1)


def neighbours():
    me = lax.axis_index("tensor")
    y, x = me // 2, me % 2
    up, down, far = ((y + d) % 4 * 2 + x for d in (1, 3, 2))
    return me, up, down, far


def across(index):
    return index // 2 * 2 + 1 - index % 2


def greet(partners):
    barrier = pltpu.get_barrier_semaphore()
    partners = tuple(partners)
    for partner in partners:
        pl.semaphore_signal(
            barrier, inc=1, device_id=partner, device_id_type=pl.DeviceIdType.MESH
        )
    return lambda: pl.semaphore_wait(barrier, len(partners))


def rows_at(index, half=None):
    if half is None:
        return pl.ds(pl.multiple_of(index * ROWS, 16), ROWS)
    return pl.ds(pl.multiple_of(index * ROWS + half * HALF, 16), HALF)


def gather_kernel(
    tok_ref, wq_ref, wk_ref, wv_ref, wz_ref, wg_ref, pre_ref, z_ref, gates_ref, tail_ref,
    held, got_tail, w_pre, w_z, w_g, w_sem, send_sem, recv_sem,
):
    me, up, down, far = neighbours()
    loads = [
        pltpu.make_async_copy(src, dst, w_sem.at[i])
        for i, (src, dst) in enumerate(
            (
                (wq_ref, w_pre.at[:, 0:256]),
                (wk_ref, w_pre.at[:, 256:512]),
                (wv_ref, w_pre.at[:, 512:1024]),
                (wz_ref, w_z),
                (wg_ref, w_g),
            )
        )
    ]
    context = lax.axis_index("context")
    after = (context + 1) % 32
    all_here = greet(
        [{"tensor": i} for i in (up, down, across(me))]
        + [{"context": i} for i in (after, (context + 31) % 32)]
    )
    for load in loads:
        load.start()
    all_here()
    tail_copy = pltpu.make_async_remote_copy(
        src_ref=pre_ref.at[8 * ROWS - 16 : 8 * ROWS],
        dst_ref=got_tail,
        send_sem=send_sem.at[14],
        recv_sem=recv_sem.at[14],
        device_id={"context": after},
        device_id_type=pl.DeviceIdType.MESH,
    )

    def copy(k, slot, half, target, own=False):
        return pltpu.make_async_remote_copy(
            src_ref=tok_ref.at[half * HALF : half * HALF + HALF] if own else held.at[rows_at(slot, half)],
            dst_ref=held.at[rows_at(slot, half)],
            send_sem=send_sem.at[k],
            recv_sem=recv_sem.at[k],
            device_id={"tensor": target},
            device_id_type=pl.DeviceIdType.MESH,
        )

    sent = []

    def send(k, slot, half, target, own=False):
        made = copy(k, slot, half, target, own)
        made.start()
        sent.append(made)

    def arrived(k, slot, half):
        copy(k, slot, half, me).wait_recv()

    def project(slot, own=False):
        source = tok_ref if own else held.at[rows_at(slot)]
        at = rows_at(slot)

        @pl.loop(0, 4)
        def _(i):
            cols = pl.ds(pl.multiple_of(i * 256, 256), 256)
            pre_ref[at, cols] = mm(source[...], w_pre[:, cols]).astype(B16)

        @pl.loop(0, 2)
        def _(i):
            cols = pl.ds(pl.multiple_of(i * 256, 256), 256)
            z_ref[at, cols] = mm(source[...], w_z[:, cols]).astype(B16)

        gates_ref[at, :] = mm(source[...], w_g[...]).astype(B16)

        @pl.when(slot == 7)
        def _():
            tail_copy.start()

    beside, beside_down, beside_up, beside_far = (across(i) for i in (me, down, up, far))
    send(0, me, 1, up, True)
    send(2, me, 0, down, True)
    send(4, me, 0, beside, True)
    send(5, me, 1, beside, True)
    send(1, me, 0, up, True)
    send(3, me, 1, down, True)
    for load in loads:
        load.wait()
    project(me, True)
    arrived(0, down, 1)
    send(6, down, 1, beside)
    arrived(2, up, 0)
    send(7, up, 0, beside)
    arrived(4, beside, 0)
    send(10, beside, 0, up)
    arrived(1, down, 0)
    send(8, down, 0, up)
    arrived(3, up, 1)
    send(9, up, 1, down)
    arrived(5, beside, 1)
    send(11, beside, 1, down)
    project(down)
    project(up)
    project(beside)
    arrived(10, beside_down, 0)
    send(12, beside_down, 0, up)
    arrived(11, beside_up, 1)
    send(13, beside_up, 1, down)
    arrived(8, far, 0)
    arrived(9, far, 1)
    project(far)
    arrived(6, beside_down, 1)
    project(beside_down)
    arrived(7, beside_up, 0)
    project(beside_up)
    arrived(12, beside_far, 0)
    arrived(13, beside_far, 1)
    project(beside_far)
    tail_copy.wait_recv()
    tail_ref[...] = got_tail[...]

    @pl.when(context == 0)
    def _():
        tail_ref[...] = jnp.zeros_like(tail_ref)

    tail_copy.wait_send()
    for made in sent:
        made.wait_send()


def gather_project(tokens, w_query, w_key, w_value, w_gate_z, w_gates):
    total, depth = 8 * ROWS, tokens.shape[1]
    vmem = pl.BlockSpec(memory_space=pltpu.VMEM)
    hbm = pl.BlockSpec(memory_space=pl.ANY)
    return pl.pallas_call(
        gather_kernel,
        in_specs=[vmem] + [hbm] * 5,
        out_specs=[vmem] * 4,
        out_shape=[
            jax.ShapeDtypeStruct((total, 1024), B16),
            jax.ShapeDtypeStruct((total, 512), B16),
            jax.ShapeDtypeStruct((total, 128), B16),
            jax.ShapeDtypeStruct((16, 1024), B16),
        ],
        scratch_shapes=[
            pltpu.VMEM((total, depth), B16),
            pltpu.VMEM((16, 1024), B16),
            pltpu.VMEM((depth, 1024), B16),
            pltpu.VMEM((depth, 512), B16),
            pltpu.VMEM((depth, 128), B16),
            pltpu.SemaphoreType.DMA((5,)),
            pltpu.SemaphoreType.DMA((15,)),
            pltpu.SemaphoreType.DMA((15,)),
        ],
        compiler_params=pltpu.CompilerParams(
            collective_id=0, has_side_effects=True, vmem_limit_bytes=48 * 1024 * 1024
        ),
    )(tokens, w_query, w_key, w_value, w_gate_z, w_gates)


def finish_kernel(
    op_ref, os_ref, z_ref, gain_ref, state_ref, w_ref, out_ref, part, got, send_sem, recv_sem
):
    me, up, down, far = neighbours()
    beside = across(me)
    all_here = greet({"tensor": i} for i in (up, down, beside))
    width = out_ref.shape[1]

    def share(slot, row):
        at = rows_at(row)
        normed = finish_rows(op_ref[at, :], os_ref[at, :], z_ref[at, :], gain_ref[...], state_ref)

        @pl.loop(0, width // 512)
        def _(i):
            cols = pl.ds(pl.multiple_of(i * 512, 512), 512)
            part[slot, :, cols] = mm(normed, w_ref[:, cols]).astype(B16)

    halves = (slice(0, HALF), slice(HALF, ROWS))
    sent = []

    def copy(k, slot, into, half, target):
        return pltpu.make_async_remote_copy(
            src_ref=part.at[slot, halves[half]],
            dst_ref=got.at[into, halves[half]],
            send_sem=send_sem.at[k],
            recv_sem=recv_sem.at[k],
            device_id={"tensor": target},
            device_id_type=pl.DeviceIdType.MESH,
        )

    def send(k, slot, into, half, target):
        made = copy(k, slot, into, half, target)
        made.start()
        sent.append(made)

    def arrived(k, into, half):
        copy(k, 0, into, half, me).wait_recv()

    def add(k, slot, into, half):
        arrived(k, into, half)
        rows = halves[half]
        part[slot, rows, :] = (
            part[slot, rows, :].astype(F32) + got[into, rows, :].astype(F32)
        ).astype(B16)

    share(0, across(far))
    all_here()
    send(0, 0, 0, 0, down)
    send(1, 0, 0, 1, up)
    share(1, across(down))
    send(2, 1, 1, 1, beside)
    share(2, across(up))
    send(3, 2, 1, 0, beside)
    share(4, far)
    share(3, beside)
    add(0, 1, 0, 0)
    send(4, 1, 2, 0, down)
    add(1, 2, 0, 1)
    send(5, 2, 2, 1, up)
    share(5, down)
    share(6, up)
    share(7, me)
    send(8, 4, 4, 0, down)
    send(9, 4, 4, 1, up)
    add(4, 3, 2, 0)
    send(6, 3, 3, 0, beside)
    add(5, 3, 2, 1)
    send(7, 3, 3, 1, beside)
    add(2, 5, 1, 1)
    send(11, 5, 5, 1, down)
    add(3, 6, 1, 0)
    send(12, 6, 6, 0, up)
    add(8, 5, 4, 0)
    send(10, 5, 5, 0, down)
    add(9, 6, 4, 1)
    send(13, 6, 6, 1, up)
    for half, ks in ((0, (6, 12, 10)), (1, (7, 11, 13))):
        for k in ks:
            arrived(k, {6: 3, 7: 3, 10: 5, 11: 5, 12: 6, 13: 6}[k], half)
        rows = halves[half]
        total = part[7, rows, :].astype(F32)
        for into in (3, 5, 6):
            total = total + got[into, rows, :].astype(F32)
        out_ref[rows, :] = total.astype(B16)
    for made in sent:
        made.wait_send()


def finish(op, os, z, gain, state, w_out):
    width = w_out.shape[1]
    vmem = pl.BlockSpec(memory_space=pltpu.VMEM)
    return pl.pallas_call(
        finish_kernel,
        in_specs=[vmem] * 6,
        out_specs=vmem,
        out_shape=jax.ShapeDtypeStruct((ROWS, width), B16),
        scratch_shapes=[
            pltpu.VMEM((8, ROWS, width), B16),
            pltpu.VMEM((7, ROWS, width), B16),
            pltpu.SemaphoreType.DMA((14,)),
            pltpu.SemaphoreType.DMA((14,)),
        ],
        compiler_params=pltpu.CompilerParams(
            collective_id=1, has_side_effects=True, vmem_limit_bytes=28 * 1024 * 1024
        ),
    )(op, os, z, gain, state, w_out)


def scan_kernel(
    x_ref, state_ref, local, pair, ring, total, before, give, back, send_sem, recv_sem
):
    me = lax.axis_index("context")
    core, z, half = me % 2, me // 2 % 8, me // 16

    def at(new_z):
        return (half * 8 + (new_z + 8) % 8) * 2 + core

    above, below = at(z + 1), at(z - 1)
    other_core = me + 1 - 2 * core
    other_half = me + 16 - 32 * half
    all_here = greet({"context": i} for i in (above, below, other_core, other_half))
    mine, theirs = pl.ds(core * 2, 2), pl.ds(2 - core * 2, 2)

    def copy(k, src, dst, target):
        return pltpu.make_async_remote_copy(
            src_ref=src,
            dst_ref=dst,
            send_sem=send_sem.at[k],
            recv_sem=recv_sem.at[k],
            device_id={"context": target},
            device_id_type=pl.DeviceIdType.MESH,
        )

    local[...] = x_ref[...].astype(B16)
    all_here()
    swap = copy(0, local.at[theirs], pair, other_core)
    swap.start()
    swap.wait_recv()
    first_core = core == 0
    firsts = []
    sent = [swap]
    no_add = jnp.zeros((DK, DK), F32)

    def apply(second, first):
        added = jnp.concatenate([no_add, second[:, DK:].astype(F32)], axis=1)
        return mm(second[:, :DK], first) + added

    def slot(distance, i):
        return ring.at[(z + distance + 8) % 8, i]

    def send(k, distance, i, target):
        made = copy(k, slot(distance, i), slot(distance, i), target)
        made.start()
        sent.append(made)

    def arrived(k, distance, i):
        copy(k, slot(distance, i), slot(distance, i), other_core).wait_recv()

    for i in range(2):
        own, got = local[core * 2 + i].astype(F32), pair[i].astype(F32)
        first = jnp.where(first_core, own, got).astype(B16)
        second = jnp.where(first_core, got, own).astype(B16)
        firsts.append(first)
        ring[z, i] = apply(second, first).astype(B16)
        send(1 + i, 0, i, above)
        send(3 + i, 0, i, below)
    for step in (1, 2, 3):
        for i in range(2):
            arrived(4 * step - 3 + i, -step, i)
            arrived(4 * step - 1 + i, step, i)
            if step < 3 or i == 0:
                send(4 * step + 1 + i, -step, i, above)
            if step < 3 or i == 1:
                send(4 * step + 3 + i, step, i, below)
    arrived(13, 4, 0)
    arrived(16, 4, 1)
    start = lax.broadcasted_iota(jnp.int32, (DK, 2 * DK), 0) == lax.broadcasted_iota(
        jnp.int32, (DK, 2 * DK), 1
    )
    runs = [start.astype(F32)] * 2
    folded = runs
    for chip in range(8):
        folded = [jnp.where(z == chip, run, here) for run, here in zip(runs, folded)]
        runs = [apply(ring[chip, i], runs[i].astype(B16)) for i in range(2)]
    for i in range(2):
        total[i] = runs[i][:, DK:].astype(B16)
    onward = copy(17, total, before, other_half)

    @pl.when(half == 0)
    def _():
        before[...] = jnp.zeros_like(before)
        onward.start()
        onward.wait_send()

    @pl.when(half == 1)
    def _():
        onward.wait_recv()

    entering = [mm(x[:, :DK].astype(B16), before[i]) + x[:, DK:] for i, x in enumerate(folded)]
    later = [
        mm(first[:, :DK], x.astype(B16)) + first[:, DK:].astype(F32)
        for first, x in zip(firsts, entering)
    ]
    for i in range(2):
        state_ref[core * 2 + i] = jnp.where(first_core, entering[i], later[i]).astype(B16)
        give[i] = jnp.where(first_core, later[i], entering[i]).astype(B16)
    swap_back = copy(18, give, back, other_core)
    swap_back.start()
    swap_back.wait()
    for i in range(2):
        state_ref[2 - core * 2 + i] = back[i]
    for made in sent:
        made.wait_send()


def entering_state(x):
    vmem = pl.BlockSpec(memory_space=pltpu.VMEM)
    return pl.pallas_call(
        scan_kernel,
        in_specs=[vmem],
        out_specs=vmem,
        out_shape=jax.ShapeDtypeStruct((HEADS, DK, DV), B16),
        scratch_shapes=[
            pltpu.VMEM((HEADS, DK, 2 * DK), B16),
            pltpu.VMEM((2, DK, 2 * DK), B16),
            pltpu.VMEM((8, 2, DK, 2 * DK), B16),
            pltpu.VMEM((2, DK, DV), B16),
            pltpu.VMEM((2, DK, DV), B16),
            pltpu.VMEM((2, DK, DV), B16),
            pltpu.VMEM((2, DK, DV), B16),
            pltpu.SemaphoreType.DMA((19,)),
            pltpu.SemaphoreType.DMA((19,)),
        ],
        compiler_params=pltpu.CompilerParams(
            collective_id=2, has_side_effects=True, vmem_limit_bytes=8 * 1024 * 1024
        ),
    )(x)


def gate_weights(w_gates):
    order = w_gates.transpose(0, 2, 1).reshape(w_gates.shape[0], 2 * HEADS)
    return jnp.pad(order, ((0, 0), (0, 128 - 2 * HEADS)))


def small_inputs(conv_query, conv_key, conv_value, a_log, dt_bias, norm_gain):
    taps = jnp.concatenate([conv_query, conv_key, conv_value], axis=1).astype(F32)
    taps = jnp.pad(taps, ((0, 8 - KW), (0, 0)))
    par = jnp.pad(jnp.stack([a_log, dt_bias]), ((0, 6), (0, 128 - HEADS)))
    return taps, par, norm_gain.astype(F32)[None, :]


def per_device(
    tokens,
    w_query,
    w_key,
    w_value,
    w_gate_z,
    w_gates,
    conv_query,
    conv_key,
    conv_value,
    a_log,
    dt_bias,
    norm_gain,
    w_out,
):
    taps, par, gain = small_inputs(conv_query, conv_key, conv_value, a_log, dt_bias, norm_gain)
    pre, z, gates, tail = gather_project(
        tokens, w_query, w_key, w_value, w_gate_z, gate_weights(w_gates)
    )
    op, os, x = local_pass(pre, tail, gates, taps, par)
    state = entering_state(x)
    return finish(op, os, z, gain, state, w_out)


def solution(mesh):
    placed = (
        P(("context", "tensor"), None),
        P(None, "tensor"),
        P(None, "tensor"),
        P(None, "tensor"),
        P(None, "tensor"),
        P(None, "tensor", None),
        P(None, "tensor"),
        P(None, "tensor"),
        P(None, "tensor"),
        P("tensor"),
        P("tensor"),
        P(),
        P("tensor", None),
    )
    return jax.shard_map(
        per_device,
        mesh=mesh,
        in_specs=placed,
        out_specs=P(("context", "tensor"), None),
        check_vma=False,
    )
```
